32 devices in a mesh: dp: 8 (over y, x, core), mp: 4 (over z).
Axes of the slice: x: 2, y: 2, z: 4, core: 2. Of those that a mesh axis runs over, the one named last changes fastest.
Arguments:
- tokens: bfloat16 [16384, 768], P('dp'), may hold values from -6 to 6
- cotangent: bfloat16 [16384, 768], P('dp'), may hold values from -6 to 6
- resets: int32 [32], P('dp'), may hold values from 0 to 1, as said below
- key_mask: int32 [16384], P('dp'), may hold values from 0 to 1, as said below
- truncation_segments: int32 [1], replicated, may hold values from 1 to 3
- qkv_weight: bfloat16 [3, 768, 768], P(None, 'dp', 'mp'), may hold values from -0.21875 to 0.21875
- out_weight: bfloat16 [768, 768], P('mp', 'dp'), may hold values from -1.5 to 1.5
- up_weight: bfloat16 [768, 3072], P('dp', 'mp'), may hold values from -0.21875 to 0.21875
- down_weight: bfloat16 [3072, 768], P('mp', 'dp'), may hold values from -0.109375 to 0.109375
- memory_init: bfloat16 [20, 768], P(None, 'dp'), may hold values from -6 to 6
- norm1_gain: bfloat16 [768], P('dp'), may hold values from 0.5 to 1.5
- first_norm_bias: bfloat16 [768], P('dp'), may hold values from -3 to 3
- norm2_gain: bfloat16 [768], P('dp'), may hold values from 0.5 to 1.5
- norm2_bias: bfloat16 [768], P('dp'), may hold values from -3 to 3
Outputs:
- layer_out: bfloat16 [16384, 768], P('dp')
- input_grad: float32 [16384, 768], P('dp', 'mp')
- qkv_grad: float32 [3, 768, 768], P(None, 'dp', 'mp')
- out_grad: float32 [768, 768], P('mp', 'dp')
- up_grad: float32 [768, 3072], P('dp', 'mp')
- down_grad: float32 [3072, 768], P('mp', 'dp')
- memory_init_gradient: float32 [20, 768], P(None, 'dp')
- norm1_gain_grad: float32 [768], P('dp')
- norm1_bias_grad: float32 [768], P('dp')
- norm2_gain_grad: float32 [768], P('dp')
- norm2_bias_grad: float32 [768], P('dp')
The draws below stay inside these ranges and needn't reach their ends.
Inputs may be any that keep to these rules, and one draw needn't show every extreme that they name: `resets`: 1 marks a segment that starts a document; entries at multiples of 4 are 1, entries at odd indices and at indices 2 more than a multiple of 4 are 0, so every document spans two or more segments and the first of each aligned group four or more. `key_mask`: within each segment of 512 positions the ones come first; only a document's last segment (followed by a 1 in resets, or at the end of an aligned group of 4 segments) has zeros, and it keeps a one.
All inputs are finite; a program needn't handle non-finite values.
Results may differ from the reference program's by a relative error of at most 0.025.
Values may be sent and summed in bfloat16 or wider, within the bound.
A program may use at most 192 MiB of HBM per device.

```python
import jax
import jax.numpy as jnp
from jax import lax

D = 768
H = 12
HD = 64
FF = 3072
SEG = 512
MEM = 20
SEGMENTS_PER_DATA = 4
TOTAL_SEGMENTS = 32
TOKENS = 16384


def layout_draw(key):
    number_of_accelerators = TOTAL_SEGMENTS // SEGMENTS_PER_DATA
    pair_count = SEGMENTS_PER_DATA // 2
    starts = jax.random.randint(jax.random.fold_in(key, 11), (number_of_accelerators, pair_count), 0, 2)
    leading = jnp.arange(pair_count)[None, :] == 0
    second = jnp.arange(pair_count)[None, :] == 1
    pair_flags = jnp.where(leading, 1, jnp.where(second, 0, starts)).astype(jnp.int32)
    reset_flags = jnp.stack([pair_flags, jnp.zeros_like(pair_flags)], axis=2).reshape(number_of_accelerators, SEGMENTS_PER_DATA)
    following = jnp.concatenate([reset_flags[:, 1:], jnp.ones((number_of_accelerators, 1), jnp.int32)], axis=1)
    lengths = jax.random.randint(jax.random.fold_in(key, 12), (number_of_accelerators, SEGMENTS_PER_DATA), 1, SEG + 1)
    filled = jnp.where(following > 0, lengths, SEG)
    keep_mask = (jnp.arange(SEG)[None, None, :] < filled[:, :, None]).astype(jnp.int32)
    return (reset_flags.reshape(number_of_accelerators * SEGMENTS_PER_DATA), keep_mask.reshape(number_of_accelerators * SEGMENTS_PER_DATA * SEG))


def draw_resets(key, part):
    return layout_draw(key)[0]


def draw_key_mask(key, part):
    return layout_draw(key)[1]


def levels(own_key, shape, pieces, low, largest):
    def one(dim, parts):
        draws = jax.random.uniform(jax.random.fold_in(jax.random.fold_in(own_key, 6), dim), (parts,), jnp.float32, low / len(pieces), largest / len(pieces))
        return jnp.repeat(jnp.exp(draws), shape[dim] // parts).reshape((-1,) + (1,) * (len(shape) - dim - 1))

    level = one(*pieces[0])
    for cut in pieces[1:]:
        level = level * one(*cut)
    return level


def scatter_about(stream_key, extent, deviation, reach, split=(), kind=jnp.bfloat16):
    values = jax.random.normal(stream_key, extent, jnp.float32) * deviation
    if len(split) > 0:
        values = levels(stream_key, extent, split, -0.22, 0.18) * values
    return jnp.clip(values, min=-reach, max=reach).astype(kind)


def setup_inputs(seed: int = 0) -> dict:
    arg_keys = jax.random.split(jax.random.key(seed), 15)
    return {
        "tokens": scatter_about(arg_keys[0], (TOKENS, D), 1.0, 6.0, ((0, 8),)),
        "cotangent": scatter_about(arg_keys[1], (TOKENS, D), 1.0, 6.0, ((0, 8),)),
        "resets": draw_resets(jax.random.fold_in(arg_keys[14], 71), 0),
        "key_mask": draw_key_mask(jax.random.fold_in(arg_keys[14], 71), 0),
        "truncation_segments": jax.random.randint(arg_keys[4], (1,), 1, SEGMENTS_PER_DATA).astype(jnp.int32),
        "qkv_weight": scatter_about(arg_keys[5], (3, D, D), D ** -0.5, 0.21875, ((1, 8), (2, 4))),
        "out_weight": scatter_about(arg_keys[6], (D, D), (HD // 4) ** -0.5, 1.5, ((0, 4), (1, 8))),
        "up_weight": scatter_about(arg_keys[7], (D, FF), D ** -0.5, 0.21875, ((0, 8), (1, 4))),
        "down_weight": scatter_about(arg_keys[8], (FF, D), FF ** -0.5, 0.109375, ((0, 4), (1, 8))),
        "memory_init": scatter_about(arg_keys[9], (MEM, D), 1.0, 6.0, ((1, 8),)),
        "norm1_gain": jnp.clip(1.0 + 0.1 * jax.random.normal(arg_keys[10], (D,), jnp.float32), 0.5, 1.5).astype(jnp.bfloat16),
        "first_norm_bias": scatter_about(arg_keys[11], (D,), 0.5, 3.0, ((0, 8),)),
        "norm2_gain": jnp.clip(1.0 + 0.1 * jax.random.normal(arg_keys[12], (D,), jnp.float32), 0.5, 1.5).astype(jnp.bfloat16),
        "norm2_bias": scatter_about(arg_keys[13], (D,), 0.5, 3.0, ((0, 8),)),
    }


EPSILON = 1e-05
PRECISE = lax.Precision.HIGHEST

@jax.custom_vjp
def low(v):
    return lax.optimization_barrier(v.astype(jnp.bfloat16)).astype(jnp.float32)

@jax.custom_vjp
def low_back(v):
    return v

def low_keep(v):
    return (low(v), None)

def low_pass(kept, grad):
    return (grad,)

def back_keep(v):
    return (v, None)

def back_low(kept, grad):
    return (low(grad),)
low.defvjp(low_keep, low_pass)
low_back.defvjp(back_keep, back_low)

def normalize(resid, gain, shift):
    center = resid - lax.optimization_barrier(jnp.mean(resid, axis=-1, keepdims=True))
    variance = lax.optimization_barrier(jnp.mean(center * center, axis=-1, keepdims=True))
    return center * lax.rsqrt(variance + EPSILON) * gain + shift

def segment_layer(hidden, valid_keys, attend_matrix, output_matrix, raise_matrix, lower_matrix, gain_one, shift_one, gain_two, shift_two):
    row_count = hidden.shape[0]
    hidden_low = low(hidden)

    def head_split(matrix):
        product = jnp.dot(hidden_low, matrix, precision=PRECISE)
        return low(low_back(product)).reshape(row_count, H, HD)
    queries = head_split(attend_matrix[0])
    key_heads = head_split(attend_matrix[1])
    value_heads = head_split(attend_matrix[2])
    scores = low_back(HD ** (-0.5) * jnp.einsum('qhd,khd->hqk', queries, key_heads, precision=PRECISE))
    scores = jnp.where(valid_keys[None, None, :] > 0, scores, -1e+30)
    attn_probs = jax.nn.softmax(scores, axis=-1)
    mixed_heads = jnp.einsum('hqk,khd->qhd', low(attn_probs), value_heads, precision=PRECISE).reshape(row_count, H * HD)
    mixed_heads = low(low_back(mixed_heads))
    attention_result = low_back(jnp.dot(mixed_heads, output_matrix, precision=PRECISE))
    norm_one = normalize(hidden + attention_result, gain_one, shift_one)
    inner_act = low_back(jnp.dot(low(norm_one), raise_matrix, precision=PRECISE))
    activated = low(jax.nn.gelu(inner_act, approximate=False))
    lowered = low_back(jnp.dot(activated, lower_matrix, precision=PRECISE))
    return normalize(norm_one + lowered, gain_two, shift_two)

def reference(tokens, cotangent, resets, key_mask, truncation_segments, qkv_weight, out_weight, up_weight, down_weight, memory_init, norm1_gain, first_norm_bias, norm2_gain, norm2_bias):
    slot_count = resets.shape[0]
    mask_blocks = key_mask.reshape(slot_count, SEG)
    seg_index = jnp.arange(slot_count, dtype=jnp.int32)
    last_start = lax.cummax(jnp.where(resets > 0, seg_index, 0).astype(jnp.int32), axis=0)
    position = (seg_index - last_start).astype(jnp.int32)
    cut_flags = jnp.where((resets == 0) & (position % truncation_segments[0] == 0), 1, 0).astype(jnp.int32)

    def chain(feed, cuts, token_values, attend_matrix, output_matrix, raise_matrix, lower_matrix, memory_start, gain_one, shift_one, gain_two, shift_two):
        token_blocks = token_values.reshape(slot_count, SEG, D)

        def advance(memory, segment_item):
            token_block, reset_flag, cut_flag, block_mask, fed = segment_item
            memory_in = jnp.where(reset_flag > 0, memory_start, jnp.where(cut_flag > 0, fed, memory))
            hidden = jnp.concatenate([memory_in, token_block], axis=0)
            valid_keys = jnp.concatenate([jnp.ones((MEM,), jnp.int32), block_mask], axis=0)
            final_rows = segment_layer(hidden, valid_keys, attend_matrix, output_matrix, raise_matrix, lower_matrix, gain_one, shift_one, gain_two, shift_two)
            return (final_rows[:MEM], (final_rows[MEM:], memory))
        initial = jnp.zeros((MEM, D), jnp.float32)
        _, (outputs, carried) = lax.scan(jax.checkpoint(advance), initial, (token_blocks, resets, cuts, mask_blocks, feed))
        return (outputs.reshape(slot_count * SEG, D), carried)
    primals = (tokens.astype(jnp.float32), qkv_weight.astype(jnp.float32), out_weight.astype(jnp.float32), up_weight.astype(jnp.float32), down_weight.astype(jnp.float32), memory_init.astype(jnp.float32), norm1_gain.astype(jnp.float32), first_norm_bias.astype(jnp.float32), norm2_gain.astype(jnp.float32), norm2_bias.astype(jnp.float32))
    empty_feed = jnp.zeros((slot_count, MEM, D), jnp.float32)
    no_cuts = jnp.zeros((slot_count,), jnp.int32)
    _, carried_memory = chain(empty_feed, no_cuts, *primals)

    def forward(*values):
        return chain(carried_memory, cut_flags, *values)[0]
    outputs, pullback = jax.vjp(forward, *primals)
    gradients = pullback(cotangent.astype(jnp.float32))
    return (outputs.astype(jnp.bfloat16), gradients[0], gradients[1], gradients[2], gradients[3], gradients[4], gradients[5], gradients[6], gradients[7], gradients[8], gradients[9])
```

```python
import functools

import jax
import jax.numpy as jnp
from jax import lax
from jax.experimental import pallas as pl
from jax.experimental.pallas import tpu as pltpu
from jax.sharding import PartitionSpec as P

HD = 64
SEG = 512
MEM = 20
PAD = 32
ROWS = SEG + PAD
EPSILON = 1e-05
MESH = pl.DeviceIdType.MESH
F32 = jnp.float32
BF16 = jnp.bfloat16


def nn(a, b):
    return lax.dot_general(a, b, (((1,), (0,)), ((), ())), preferred_element_type=F32)


def nt(a, b):
    return lax.dot_general(a, b, (((1,), (1,)), ((), ())), preferred_element_type=F32)


def tn(a, b):
    return lax.dot_general(a, b, (((0,), (0,)), ((), ())), preferred_element_type=F32)


def normalize(resid):
    center = resid - jnp.mean(resid, axis=-1, keepdims=True)
    inverse = lax.rsqrt(jnp.mean(center * center, axis=-1, keepdims=True) + EPSILON)
    return center * inverse, inverse


def normalize_back(grad_out, hat, inverse, gain):
    grad_hat = grad_out * gain
    return inverse * (
        grad_hat
        - jnp.mean(grad_hat, axis=-1, keepdims=True)
        - hat * jnp.mean(grad_hat * hat, axis=-1, keepdims=True)
    )


def layer_kernel(
    n,
    tok_hbm, cot_hbm, flags, kbias, norms, mem_init, wqkv_hbm, wot_hbm, wup_hbm, wdnt_hbm,
    lo_hbm, dx_hbm, dqkv_hbm, dot_hbm, dup_hbm, ddnt_hbm, dmem, dnorm,
    wqkv, wot, wup, wdnt, hid, cot, qkv, probs, mixed, hat1, inv1, nlow, act, slope, hat2, inv2, lout,
    g2low, ginner, gone, g1low, gmix, dk32, dv32, dqkv, dxs,
    mem_recv, mem_send, gm_recv, gm_send,
    load_sem, w_sem, lo_sem, dx_sem, lo_send, lo_recv, dx_send, dx_recv, chain_sem,
):
    dp = lax.axis_index("dp")
    mp = lax.axis_index("mp")
    width = hid.shape[1]
    pairs = width // 128
    parts = wup.shape[0]
    tok_rows = pl.ds(0, SEG)
    mem_rows = pl.ds(SEG, PAD)

    load_tok = pltpu.make_async_copy(
        tok_hbm.at[pl.ds(mp * SEG, SEG)], hid.at[tok_rows], load_sem.at[0]
    )
    load_cot = pltpu.make_async_copy(cot_hbm.at[pl.ds(mp * SEG, SEG)], cot, load_sem.at[1])
    load_tok.start()
    loads = [
        pltpu.make_async_copy(src, dst, w_sem.at[i])
        for i, (src, dst) in enumerate(
            ((wqkv_hbm, wqkv), (wot_hbm, wot), (wup_hbm, wup), (wdnt_hbm, wdnt))
        )
    ]
    for load in loads:
        load.start()
    load_cot.start()

    @pl.when(mp == 0)
    def _():
        mem_recv[...] = jnp.zeros_like(mem_recv)

    @pl.when(mp == n - 1)
    def _():
        gm_recv[...] = jnp.zeros_like(gm_recv)

    barrier = pltpu.get_barrier_semaphore()
    for step in range(1, n):
        pl.semaphore_signal(
            barrier, inc=1, device_id=(dp, lax.rem(mp + step, n)), device_id_type=MESH
        )
    pl.semaphore_wait(barrier, n - 1)

    gain1, bias1 = norms[0:1], norms[1:2]
    gain2, bias2 = norms[2:3], norms[3:4]
    lane = lax.broadcasted_iota(jnp.int32, (1, 128), 1)
    half_scaled = [
        jnp.where(lane < HD, HD**-0.5, 0.0).astype(BF16),
        jnp.where(lane < HD, 0.0, HD**-0.5).astype(BF16),
    ]
    half_one = [
        jnp.where(lane < HD, 1.0, 0.0).astype(BF16),
        jnp.where(lane < HD, 0.0, 1.0).astype(BF16),
    ]

    def project(rows):
        x = hid[rows, :]
        for g in range(3):
            qkv[g, rows, :] = nn(x, wqkv[g]).astype(BF16)

    def attend(rows, count):
        @pl.loop(0, pairs)
        def _(pair):
            lanes = pl.ds(pl.multiple_of(pair * 128, 128), 128)
            q = qkv[0, rows, lanes]
            k = qkv[1, :, lanes]
            v = qkv[2, :, lanes]
            outs = []
            for half in range(2):
                scores = nt(q * half_scaled[half], k) + kbias[...]
                top = jnp.max(scores, axis=-1, keepdims=True)
                e = jnp.exp(scores - top)
                p = (e * (1.0 / jnp.sum(e, axis=-1, keepdims=True))).astype(BF16)
                probs[2 * pair + half, rows, :] = p
                outs.append(nn(p, v))
            first = lax.broadcasted_iota(jnp.int32, (count, 128), 1) < HD
            mixed[rows, lanes] = jnp.where(first, outs[0], outs[1]).astype(BF16)

    def feed(rows):
        resid = hid[rows, :].astype(F32) + nt(mixed[rows, :], wot[...])
        h1, i1 = normalize(resid)
        hat1[rows, :] = h1
        inv1[rows, :] = i1
        norm_one = h1 * gain1 + bias1
        nlow[rows, :] = norm_one.astype(BF16)
        hat2[rows, :] = norm_one

        @pl.loop(0, parts)
        def _(j):
            inner = nn(nlow[rows, :], wup[j])
            cumulative = 0.5 * (1.0 + lax.erf(inner * 0.7071067811865476))
            density = jnp.exp(-0.5 * inner * inner) * 0.3989422804014327
            a = (inner * cumulative).astype(BF16)
            act[j, rows, :] = a
            slope[j, rows, :] = (cumulative + inner * density).astype(BF16)
            hat2[rows, :] += nt(a, wdnt[j])

        h2, i2 = normalize(hat2[rows, :])
        hat2[rows, :] = h2
        inv2[rows, :] = i2
        return (h2 * gain2 + bias2).astype(BF16)

    def feed_back(rows, grad_final):
        h2 = hat2[rows, :]
        dnorm[2:3, :] += jnp.sum(grad_final * h2, axis=0, keepdims=True)
        dnorm[3:4, :] += jnp.sum(grad_final, axis=0, keepdims=True)
        g2 = normalize_back(grad_final, h2, inv2[rows, :], gain2)
        g2low[rows, :] = g2.astype(BF16)
        gone[rows, :] = g2

        @pl.loop(0, parts)
        def _(j):
            gi = (nn(g2low[rows, :], wdnt[j]) * slope[j, rows, :].astype(F32)).astype(BF16)
            ginner[j, rows, :] = gi
            gone[rows, :] += nt(gi, wup[j])

        grad_norm = gone[rows, :]
        h1 = hat1[rows, :]
        dnorm[0:1, :] += jnp.sum(grad_norm * h1, axis=0, keepdims=True)
        dnorm[1:2, :] += jnp.sum(grad_norm, axis=0, keepdims=True)
        g1 = normalize_back(grad_norm, h1, inv1[rows, :], gain1)
        gone[rows, :] = g1
        low = g1.astype(BF16)
        g1low[rows, :] = low
        gmix[rows, :] = nn(low, wot[...]).astype(BF16)

    def attend_back(rows, count, first_time):
        @pl.loop(0, pairs)
        def _(pair):
            lanes = pl.ds(pl.multiple_of(pair * 128, 128), 128)
            q = qkv[0, rows, lanes]
            k = qkv[1, :, lanes]
            v = qkv[2, :, lanes]
            g = gmix[rows, lanes]
            dqs = []
            dk = None
            dv = None
            for half in range(2):
                p = probs[2 * pair + half, rows, :]
                gh = g * half_one[half]
                dprob = nt(gh, v)
                pf = p.astype(F32)
                delta = jnp.sum(pf * dprob, axis=-1, keepdims=True)
                ds = (pf * (dprob - delta)).astype(BF16)
                dv_h = tn(p, gh)
                dk_h = tn(ds, q * half_scaled[half])
                dqs.append(nn(ds, k))
                dk = dk_h if dk is None else dk + dk_h
                dv = dv_h if dv is None else dv + dv_h
            first = lax.broadcasted_iota(jnp.int32, (count, 128), 1) < HD
            dqkv[0, rows, lanes] = (jnp.where(first, dqs[0], dqs[1]) * HD**-0.5).astype(BF16)
            if first_time:
                dk32[:, lanes] = dk
                dv32[:, lanes] = dv
            else:
                dk32[:, lanes] += dk
                dv32[:, lanes] += dv

    def chain_copy(src, dst, slot, peer):
        return pltpu.make_async_remote_copy(
            src_ref=src, dst_ref=dst,
            send_sem=chain_sem.at[2 * slot], recv_sem=chain_sem.at[2 * slot + 1],
            device_id=(dp, peer), device_id_type=MESH,
        )

    forward_copy = chain_copy(mem_send, mem_recv, 0, lax.rem(mp + 1, n))
    backward_copy = chain_copy(gm_send, gm_recv, 1, lax.rem(mp + n - 1, n))

    load_tok.wait()
    loads[0].wait()

    @pl.loop(0, 2)
    def _(c):
        project(pl.ds(pl.multiple_of(c * 256, 256), 256))

    @pl.when(mp > 0)
    def _():
        forward_copy.wait_recv()

    hid[mem_rows, :] = jnp.where(
        flags[0:1, 0:1] > 0, mem_init[...].astype(F32), mem_recv[...].astype(F32)
    ).astype(BF16)
    project(mem_rows)
    attend(mem_rows, PAD)
    for load in loads[1:]:
        load.wait()
    mem_send[...] = feed(mem_rows)

    @pl.when(mp < n - 1)
    def _():
        forward_copy.start()

    attend(tok_rows, SEG)

    @pl.loop(0, 2)
    def _(c):
        rows = pl.ds(pl.multiple_of(c * 256, 256), 256)
        lout[rows, :] = feed(rows)

    own = pl.ds(mp * SEG, SEG)
    keep_out = pltpu.make_async_copy(lout, lo_hbm.at[own], lo_sem)
    keep_out.start()
    out_copies = []
    for step in range(1, n):
        copy = pltpu.make_async_remote_copy(
            src_ref=lout, dst_ref=lo_hbm.at[own],
            send_sem=lo_send.at[step - 1], recv_sem=lo_recv.at[step - 1],
            device_id=(dp, lax.rem(mp + step, n)), device_id_type=MESH,
        )
        copy.start()
        out_copies.append(copy)

    dnorm[...] = jnp.zeros_like(dnorm)
    load_cot.wait()

    @pl.loop(0, 2)
    def _(c):
        rows = pl.ds(pl.multiple_of(c * 256, 256), 256)
        feed_back(rows, cot[rows, :].astype(F32))

    attend_back(tok_rows, SEG, True)

    @pl.when(mp < n - 1)
    def _():
        backward_copy.wait_recv()

    feed_back(mem_rows, gm_recv[...].astype(F32))
    attend_back(mem_rows, PAD, False)

    def input_grad(rows):
        return (
            gone[rows, :]
            + nt(dqkv[0, rows, :], wqkv[0])
            + nt(dqkv[1, rows, :], wqkv[1])
            + nt(dqkv[2, rows, :], wqkv[2])
        )

    dqkv[1, :, :] = dk32[...].astype(BF16)
    dqkv[2, :, :] = dv32[...].astype(BF16)
    gmem = input_grad(mem_rows)
    gm_send[...] = jnp.where(flags[1:2, 0:1] > 0, gmem, 0.0).astype(BF16)

    @pl.when(mp > 0)
    def _():
        backward_copy.start()

    dmem[...] = jnp.where(flags[0:1, 0:1] > 0, gmem, 0.0)

    cols = width // n

    @pl.loop(0, 2)
    def _(c):
        rows = pl.ds(pl.multiple_of(c * 256, 256), 256)
        g = input_grad(rows).astype(BF16)
        for j in range(n):
            dxs[j, rows, :] = g[:, j * cols : (j + 1) * cols]

    keep_dx = pltpu.make_async_copy(dxs.at[mp], dx_hbm.at[mp], dx_sem)
    keep_dx.start()
    dx_copies = []
    for step in range(1, n):
        peer = lax.rem(mp + step, n)
        copy = pltpu.make_async_remote_copy(
            src_ref=dxs.at[peer], dst_ref=dx_hbm.at[mp],
            send_sem=dx_send.at[step - 1], recv_sem=dx_recv.at[step - 1],
            device_id=(dp, peer), device_id_type=MESH,
        )
        copy.start()
        dx_copies.append(copy)

    @pl.loop(0, parts)
    def _(j):
        wdnt[j] = tn(g2low[...], act[j]).astype(BF16)

    @pl.loop(0, parts)
    def _(j):
        wup[j] = tn(nlow[...], ginner[j]).astype(BF16)

    wot[...] = tn(g1low[...], mixed[...]).astype(BF16)

    @pl.loop(0, 3)
    def _(g):
        wqkv[g] = tn(hid[...], dqkv[g]).astype(BF16)

    stores = [
        pltpu.make_async_copy(src, dst, w_sem.at[i])
        for i, (src, dst) in enumerate(
            ((wqkv, dqkv_hbm), (wot, dot_hbm), (wup, dup_hbm), (wdnt, ddnt_hbm))
        )
    ]
    for store in stores:
        store.start()
    for store in stores:
        store.wait()
    keep_out.wait()
    keep_dx.wait()
    for copy in out_copies + dx_copies:
        copy.wait()

    @pl.when(mp < n - 1)
    def _():
        forward_copy.wait_send()

    @pl.when(mp > 0)
    def _():
        backward_copy.wait_send()


def run_layer(n, tokens, cotangent, flags, kbias, norms, mem_init, wqkv, wot, wup, wdnt):
    width = tokens.shape[1]
    parts = wup.shape[0]
    heads = width // HD
    vmem = pl.BlockSpec(memory_space=pltpu.VMEM)
    anyspace = pl.BlockSpec(memory_space=pl.ANY)
    out_shape = (
        jax.ShapeDtypeStruct((n * SEG, width), BF16),
        jax.ShapeDtypeStruct((n, SEG, width // n), BF16),
        jax.ShapeDtypeStruct(wqkv.shape, BF16),
        jax.ShapeDtypeStruct(wot.shape, BF16),
        jax.ShapeDtypeStruct(wup.shape, BF16),
        jax.ShapeDtypeStruct(wdnt.shape, BF16),
        jax.ShapeDtypeStruct((PAD, width), F32),
        jax.ShapeDtypeStruct((8, width), F32),
    )
    row_bf = pltpu.VMEM((ROWS, width), BF16)
    row_f = pltpu.VMEM((ROWS, width), F32)
    one_f = pltpu.VMEM((ROWS, 1), F32)
    wide = pltpu.VMEM((parts, ROWS, width), BF16)
    mem_bf = pltpu.VMEM((PAD, width), BF16)
    sems = pltpu.SemaphoreType.DMA
    return pl.pallas_call(
        functools.partial(layer_kernel, n),
        out_shape=out_shape,
        in_specs=[anyspace] * 2 + [vmem] * 4 + [anyspace] * 4,
        out_specs=(anyspace,) * 6 + (vmem,) * 2,
        scratch_shapes=[
            pltpu.VMEM(wqkv.shape, BF16), pltpu.VMEM(wot.shape, BF16),
            pltpu.VMEM(wup.shape, BF16), pltpu.VMEM(wdnt.shape, BF16),
            row_bf, pltpu.VMEM((SEG, width), BF16), pltpu.VMEM((3, ROWS, width), BF16),
            pltpu.VMEM((heads, ROWS, ROWS), BF16), row_bf, row_f, one_f, row_bf, wide, wide, row_f,
            one_f, pltpu.VMEM((SEG, width), BF16),
            row_bf, wide, row_f, row_bf, row_bf, row_f, row_f, pltpu.VMEM((3, ROWS, width), BF16),
            pltpu.VMEM((n, SEG, width // n), BF16),
            mem_bf, mem_bf, mem_bf, mem_bf,
            sems((2,)), sems((4,)), sems, sems, sems((n - 1,)), sems((n - 1,)), sems((n - 1,)), sems((n - 1,)),
            sems((4,)),
        ],
        compiler_params=pltpu.CompilerParams(
            collective_id=0, has_side_effects=True, vmem_limit_bytes=62 * 2**20
        ),
        cost_estimate=pl.CostEstimate(
            flops=26_000_000_000, bytes_accessed=40_000_000, transcendentals=10_000_000
        ),
    )(tokens, cotangent, flags, kbias, norms, mem_init, wqkv, wot, wup, wdnt)


def shards(
    tokens, cotangent, resets, key_mask, truncation_segments, qkv_weight, out_weight, up_weight,
    down_weight, memory_init, norm1_gain, first_norm_bias, norm2_gain, norm2_bias,
):
    n = lax.axis_size("mp")
    m = lax.axis_size("dp")
    mp = lax.axis_index("mp")
    dp = lax.axis_index("dp")
    width = tokens.shape[1]
    slots = resets.shape[0]
    rows = width // m
    cols = width // n
    block = jnp.concatenate([qkv_weight, out_weight.T[None]], axis=0)
    block = lax.all_gather(block, ("mp", "dp"), axis=0)
    block = block.reshape(n, m, 4, rows, cols).transpose(2, 1, 3, 0, 4).reshape(4, width, width)
    wup = lax.all_gather(up_weight, ("mp", "dp"), axis=0).reshape(n, width, -1)
    wdnt = lax.all_gather(down_weight.T, ("mp", "dp"), axis=0).reshape(n, width, -1)
    small = jnp.concatenate(
        [norm1_gain[None], first_norm_bias[None], norm2_gain[None], norm2_bias[None], memory_init],
        axis=0,
    )
    small = lax.all_gather(small, "dp", axis=1, tiled=True)
    norms = jnp.pad(small[:4].astype(F32), ((0, 4), (0, 0)))
    mem_init = jnp.pad(small[4:], ((0, PAD - MEM), (0, 0)))
    seg_index = jnp.arange(slots, dtype=jnp.int32)
    last_start = lax.cummax(jnp.where(resets > 0, seg_index, 0), axis=0)
    position = seg_index - last_start
    cut = (resets == 0) & (position % truncation_segments[0] == 0)
    carried = jnp.where((resets > 0) | cut, 0, 1)
    pair = jnp.stack([resets[mp], carried[mp]]).astype(F32)
    flags = jnp.broadcast_to(jnp.pad(pair, (0, 6))[:, None], (8, 128))
    valid = lax.dynamic_slice_in_dim(key_mask, mp * SEG, SEG, 0)
    valid = jnp.concatenate([valid, jnp.ones((MEM,), jnp.int32), jnp.zeros((PAD - MEM,), jnp.int32)])
    kbias = jnp.where(valid > 0, 0.0, -1e30).astype(F32)[None, :]

    lo, dx, dqkv, dot_w, dup, ddnt, dmem, dnorm = run_layer(
        n, tokens, cotangent, flags, kbias, norms, mem_init, block[:3], block[3], wup, wdnt
    )
    dblock = jnp.concatenate([dqkv, dot_w[None]], axis=0)
    dblock = dblock.reshape(4, m, rows, n, cols).transpose(3, 1, 0, 2, 4).reshape(n * m, 4, rows, cols)
    dblock = lax.psum_scatter(dblock, ("mp", "dp"), scatter_dimension=0).astype(F32)
    dup = lax.psum_scatter(
        dup.reshape(n * m, rows, -1), ("mp", "dp"), scatter_dimension=0
    ).astype(F32)
    ddnt = lax.psum_scatter(
        ddnt.reshape(n * m, rows, -1), ("mp", "dp"), scatter_dimension=0
    ).astype(F32)
    tiny = lax.psum(jnp.concatenate([dmem[:MEM], dnorm[:4]], axis=0), ("mp", "dp"))
    tiny = lax.dynamic_slice_in_dim(tiny, dp * rows, rows, 1)
    return (
        lo,
        dx.astype(F32).reshape(n * SEG, cols),
        dblock[:3],
        dblock[3].T,
        dup,
        ddnt.T,
        tiny[:MEM],
        tiny[MEM],
        tiny[MEM + 1],
        tiny[MEM + 2],
        tiny[MEM + 3],
    )


def solution(mesh):
    return jax.shard_map(
        shards,
        mesh=mesh,
        in_specs=(
            P("dp", None), P("dp", None), P("dp"), P("dp"), P(),
            P(None, "dp", "mp"), P("mp", "dp"), P("dp", "mp"), P("mp", "dp"), P(None, "dp"),
            P("dp"), P("dp"), P("dp"), P("dp"),
        ),
        out_specs=(
            P("dp", None), P("dp", "mp"), P(None, "dp", "mp"), P("mp", "dp"), P("dp", "mp"),
            P("mp", "dp"), P(None, "dp"), P("dp"), P("dp"), P("dp"), P("dp"),
        ),
        check_vma=False,
    )
```

```python
import functools

import jax
import jax.numpy as jnp
from jax import lax
from jax.experimental import pallas as pl
from jax.experimental.pallas import tpu as pltpu
from jax.sharding import PartitionSpec as P

HD = 64
SEG = 512
MEM = 20
PAD = 32
ROWS = SEG + PAD
PIECES = 8
EPSILON = 1e-05
MESH = pl.DeviceIdType.MESH
F32 = jnp.float32
BF16 = jnp.bfloat16


def nn(a, b):
    return lax.dot_general(a, b, (((1,), (0,)), ((), ())), preferred_element_type=F32)


def nt(a, b):
    return lax.dot_general(a, b, (((1,), (1,)), ((), ())), preferred_element_type=F32)


def tn(a, b):
    return lax.dot_general(a, b, (((0,), (0,)), ((), ())), preferred_element_type=F32)


def normalize(resid):
    center = resid - jnp.mean(resid, axis=-1, keepdims=True)
    inverse = lax.rsqrt(jnp.mean(center * center, axis=-1, keepdims=True) + EPSILON)
    return center * inverse, inverse


def normalize_back(grad_out, hat, inverse, gain):
    grad_hat = grad_out * gain
    return inverse * (
        grad_hat
        - jnp.mean(grad_hat, axis=-1, keepdims=True)
        - hat * jnp.mean(grad_hat * hat, axis=-1, keepdims=True)
    )


def place(n):
    dp = lax.axis_index("dp")
    mp = lax.axis_index("mp")
    c, x, y = lax.rem(dp, 2), lax.rem(dp // 2, 2), dp // 4
    return {
        "c": c,
        "x": x,
        "y": y,
        "mp": mp,
        "core": (dp + 1 - 2 * c, mp),
        "xp": (dp + 2 - 4 * x, mp),
        "yp": (dp + 4 - 8 * y, mp),
        "z": [mp, mp + 1 - 2 * lax.rem(mp, 2), lax.rem(mp + 2, 4), 3 - mp],
        "dp": dp,
    }


def remote(src, dst, send, recv, peer):
    return pltpu.make_async_remote_copy(
        src_ref=src, dst_ref=dst, send_sem=send, recv_sem=recv, device_id=peer, device_id_type=MESH
    )


def gather_events(at, shards_in, fulls, sems):
    z_send, z_recv, s1_send, s1_recv, s2_send, s2_recv, c_send, c_recv, own_sem = sems
    c, x, y, mp = at["c"], at["x"], at["y"], at["mp"]
    mine, by_x, by_y, diag = (y, x), (y, 1 - x), (1 - y, x), (1 - y, 1 - x)
    kinds = len(shards_in)
    sent = []
    own = []

    def go(copy):
        copy.start()
        sent.append(copy)
        return copy

    def arrived(ref, sem):
        remote(ref, ref, s1_send.at[0, 0], sem, at["core"]).wait_recv()

    def start_z(t):
        for k in range(1, 4):
            go(remote(shards_in[t], fulls[t].at[mp, *mine, c], z_send.at[t, k - 1],
                      z_recv.at[t, k - 1], (at["dp"], at["z"][k])))

    def e1(t, k):
        s = 4 * t + k
        j = at["z"][k]
        full = fulls[t]
        piece = full.at[j, *mine, c]
        if k == 0:
            keep = pltpu.make_async_copy(shards_in[t], piece, own_sem.at[t])
            keep.start()
            own.append(keep)
            src = shards_in[t]
        else:
            arrived(piece, z_recv.at[t, k - 1])
            src = piece
        go(remote(src, piece, s1_send.at[s, 0], s1_recv.at[s, 0], at["xp"]))
        go(remote(src, piece, s1_send.at[s, 1], s1_recv.at[s, 1], at["yp"]))
        go(remote(src, piece, c_send.at[s, 0], c_recv.at[s, 0], at["core"]))

    def e2(t, k):
        s = 4 * t + k
        full = fulls[t]
        j = at["z"][k]
        half = full.shape[4] // 2
        px, py = full.at[j, *by_x, c], full.at[j, *by_y, c]
        arrived(px, s1_recv.at[s, 0])
        low = full.at[j, *by_x, c, pl.ds(0, half)]
        go(remote(low, low, s2_send.at[s, 1], s2_recv.at[s, 1], at["yp"]))
        go(remote(px, px, c_send.at[s, 1], c_recv.at[s, 1], at["core"]))
        arrived(py, s1_recv.at[s, 1])
        high = full.at[j, *by_y, c, pl.ds(half, half)]
        go(remote(high, high, s2_send.at[s, 0], s2_recv.at[s, 0], at["xp"]))
        go(remote(py, py, c_send.at[s, 2], c_recv.at[s, 2], at["core"]))

    def e3(t, k):
        s = 4 * t + k
        full = fulls[t]
        j = at["z"][k]
        half = full.shape[4] // 2
        arrived(full.at[j, *diag, c, pl.ds(half, half)], s2_recv.at[s, 0])
        arrived(full.at[j, *diag, c, pl.ds(0, half)], s2_recv.at[s, 1])
        pd = full.at[j, *diag, c]
        go(remote(pd, pd, c_send.at[s, 3], c_recv.at[s, 3], at["core"]))

    def e4(t, k):
        s = 4 * t + k
        full = fulls[t]
        j = at["z"][k]
        for q, spot in enumerate((mine, by_x, by_y, diag)):
            arrived(full.at[j, *spot, 1 - c], c_recv.at[s, q])
        if k == 0:
            own[t].wait()

    events = []
    order = [(t, k) for t in range(kinds) for k in range(4)]
    total = len(order)
    for s in range(total + 3):
        def event(s=s):
            if s == 0:
                start_z(0)
            if s % 4 == 1 and s // 4 + 1 < kinds:
                start_z(s // 4 + 1)
            if s < total:
                e1(*order[s])
            if 0 <= s - 1 < total:
                e2(*order[s - 1])
            if 0 <= s - 2 < total:
                e3(*order[s - 2])
            if 0 <= s - 3 < total:
                e4(*order[s - 3])
        events.append(event)

    def finish():
        for copy in sent:
            copy.wait_send()

    return events, finish


def gather_sems(kinds):
    sems = pltpu.SemaphoreType.DMA
    total = 4 * kinds
    return [
        sems((kinds, 3)), sems((kinds, 3)), sems((total, 2)), sems((total, 2)), sems((total, 2)),
        sems((total, 2)), sems((total, 4)), sems((total, 4)), sems((kinds,)),
    ]


def scatter_steps(at, fulls, firsts, rings, r2x, r2y, r3x, r3y, r4, sems):
    c_send, c_recv, l_sem, s1_send, s1_recv, s2_send, s2_recv, z_send, z_recv = sems
    c, x, y = at["c"], at["x"], at["y"]
    order = (3, 2, 1, 0)
    sent = []

    def go(copy):
        copy.start()
        sent.append(copy)

    def arrived(ref, sem):
        remote(ref, ref, c_send.at[0], sem, at["core"]).wait_recv()

    def spot(s):
        t, q = s // 4, s % 4
        return t, q, at["z"][order[q]], fulls[t].shape[4] // 2

    def load(s):
        t, q, _, _ = spot(s)
        return pltpu.make_async_copy(firsts[t].at[q], rings[t], l_sem.at[s])

    def f1(s):
        t, q, j, _ = spot(s)
        go(remote(fulls[t].at[j, :, :, 1 - c], firsts[t].at[q], c_send.at[s], c_recv.at[s],
                  at["core"]))

    def fetch(s):
        t, q, _, _ = spot(s)
        arrived(firsts[t].at[q], c_recv.at[s])
        load(s).start()

    def add(p, q):
        return (p.astype(F32) + q.astype(F32)).astype(BF16)

    def f2(s):
        t, q, j, half = spot(s)
        full = fulls[t]
        load(s).wait()
        for yy in range(2):
            for xx in range(2):
                full[j, yy, xx, c] = add(full[j, yy, xx, c], rings[t][yy, xx])
        go(remote(full.at[j, :, 1 - x, c, pl.ds(0, half)], r2x[t].at[q],
                  s1_send.at[s, 0], s1_recv.at[s, 0], at["xp"]))
        go(remote(full.at[j, 1 - y, :, c, pl.ds(half, half)], r2y[t].at[q],
                  s1_send.at[s, 1], s1_recv.at[s, 1], at["yp"]))

    def f3(s):
        t, q, j, half = spot(s)
        full = fulls[t]
        low, high = slice(0, half), slice(half, 2 * half)
        arrived(r2x[t].at[q], s1_recv.at[s, 0])
        for v in range(2):
            full[j, v, x, c, low] = add(full[j, v, x, c, low], r2x[t][q, v])
        go(remote(full.at[j, 1 - y, x, c, pl.ds(0, half)], r3y[t].at[q],
                  s2_send.at[s, 1], s2_recv.at[s, 1], at["yp"]))
        arrived(r2y[t].at[q], s1_recv.at[s, 1])
        for v in range(2):
            full[j, y, v, c, high] = add(full[j, y, v, c, high], r2y[t][q, v])
        go(remote(full.at[j, y, 1 - x, c, pl.ds(half, half)], r3x[t].at[q],
                  s2_send.at[s, 0], s2_recv.at[s, 0], at["xp"]))

    def f4(s):
        t, q, j, half = spot(s)
        full = fulls[t]
        k = order[q]
        low, high = slice(0, half), slice(half, 2 * half)
        arrived(r3y[t].at[q], s2_recv.at[s, 1])
        arrived(r3x[t].at[q], s2_recv.at[s, 0])
        full[j, y, x, c, low] = add(full[j, y, x, c, low], r3y[t][q])
        full[j, y, x, c, high] = add(full[j, y, x, c, high], r3x[t][q])
        if k:
            go(remote(full.at[j, y, x, c], r4[t].at[k - 1], z_send.at[t, k - 1],
                      z_recv.at[t, k - 1], (at["dp"], at["z"][k])))

    def total_of(t):
        got = fulls[t][at["mp"], y, x, c].astype(F32)
        for k in range(1, 4):
            arrived(r4[t].at[k - 1], z_recv.at[t, k - 1])
            got += r4[t][k - 1].astype(F32)
        return got

    def finish():
        for copy in sent:
            copy.wait_send()

    return f1, fetch, f2, f3, f4, total_of, finish


def scatter_scratch(shapes):
    sems = pltpu.SemaphoreType.DMA
    kinds = len(shapes)
    total = 4 * kinds

    def per(f):
        return [pltpu.VMEM(f(r, w), BF16) for r, w in shapes]

    return (
        per(lambda r, w: (4, 2, r // 2, w))
        + per(lambda r, w: (4, 2, r // 2, w))
        + per(lambda r, w: (4, r // 2, w))
        + per(lambda r, w: (4, r // 2, w))
        + per(lambda r, w: (3, r, w))
        + [sems((total,)), sems((total,)), sems((total,)), sems((total, 2)), sems((total, 2)),
           sems((total, 2)), sems((total, 2)), sems((kinds, 3)), sems((kinds, 3))]
    )


def tiny_steps(at, tiny, tsum, trecv, t_send, t_recv):
    peers = [at["core"], at["xp"], at["yp"], (at["dp"], at["z"][1]), (at["dp"], at["z"][2])]

    def copy(q):
        src = tiny if q == 0 else tsum.at[(q - 1) % 2]
        return remote(src, trecv.at[q], t_send.at[q], t_recv.at[q], peers[q])

    def end(q):
        copy(q).wait()
        tsum[q % 2] = (tiny[...] if q == 0 else tsum[(q - 1) % 2]) + trecv[q]

    return (lambda q: copy(q).start()), end


def layer_kernel(n, m, fused, *refs):
    at = place(n)
    dp, mp = lax.axis_index("dp"), lax.axis_index("mp")
    take = iter(refs)

    def some(count):
        return [next(take) for _ in range(count)]

    tok_hbm, cot_hbm, resets, truncation, key_mask = some(5)
    if fused:
        norm_in, (memory_in, qkv_w, out_w, up_w, down_w) = some(4), some(5)
        lo_hbm, dx_hbm = some(2)
        firsts = some(3)
        dqkv_out, dout_out, dup_out, ddown_out, dmem_out, *dnorm_out = some(9)
        small_full, small_own, ablk = some(3)
        fulls = some(3)
        gsems = some(9)
        small_send, small_recv = some(2)
        wqkv, wot, ring_a = some(3)
        r2x, r2y, r3x, r3y, r4 = [some(3) for _ in range(5)]
        ssems = some(9)
        tiny, tsum, trecv, t_send, t_recv = some(5)
        afull, ufull, dfull = fulls
        parts = n
        width = wot.shape[0]
        wup = ufull.reshape(n, width, width)
        wdnt = dfull.reshape(n, width, width)
    else:
        small_in, weights_hbm = next(take), some(4)
        lo_hbm, dx_hbm = some(2)
        grads_hbm, tiny = some(4), next(take)
        wqkv, wot, wup, wdnt = some(4)
    (
        kbias, small, pmem, kall, vall, pmemory, stats,
        hid, cot, qkv, probs, mixed, hat1, inv, nlow, act, slope, hat2,
        g2low, g1low, gmix, dqkv, dxs, dnorm, dmem,
        mem_recv, mem_send, gm_recv, gm_send,
        load_sem, w_sem, lo_sem, dx_sem, lo_send, lo_recv, dx_send, dx_recv, chain_sem,
    ) = some(38)
    qall, gall = kall, vall
    ginner, gone, lout = slope, hat2, gmix
    if fused:
        ring_b = cot.at[pl.ds(0, 4 * up_w.shape[0])].reshape(2, 2, *up_w.shape)
        rings = (ring_b, ring_b, ring_a)
    width = hid.shape[1]
    heads = width // HD
    pairs = width // 128
    parts = n
    part = width // m
    tok_rows = pl.ds(0, SEG)
    mem_rows = pl.ds(SEG, PAD)

    load_tok = pltpu.make_async_copy(
        tok_hbm.at[pl.ds(mp * SEG, SEG)], hid.at[tok_rows], load_sem.at[0]
    )
    load_cot = pltpu.make_async_copy(cot_hbm.at[pl.ds(mp * SEG, SEG)], cot, load_sem.at[1])
    load_tok.start()
    if fused:
        for i, ref in enumerate(norm_in):
            small_own[i : i + 1, :] = ref[...].astype(F32)
        small_own[4 : 4 + MEM, :] = memory_in[...].astype(F32)
        small_own[4 + MEM :, :] = jnp.zeros((small_own.shape[0] - 4 - MEM, part), F32)
        small_full[dp] = small_own[...]
        shard = [qkv_w[0], qkv_w[1], qkv_w[2], out_w[...].T]
        for g in range(4):
            ablk[g * part : (g + 1) * part, :] = shard[g][:, :128]
        for g in range(2):
            ablk[(4 + g) * part : (5 + g) * part, :] = jnp.concatenate(
                [shard[2 * g][:, 128:], shard[2 * g + 1][:, 128:]], axis=1
            )
    last_start = jnp.int32(0)
    for t in range(n):
        last_start = jnp.where((resets[t] > 0) & (t <= mp), t, last_start)
    cut = resets[mp] < 0
    for q in range(n):
        cut = cut | (mp - last_start == q * truncation[0])
    starts = jnp.full((PAD, hid.shape[1]), jnp.where(resets[mp] > 0, 1.0, 0.0)) > 0
    carries = jnp.full((PAD, hid.shape[1]), jnp.where((resets[mp] > 0) | cut, 0.0, 1.0)) > 0
    spare = lax.broadcasted_iota(jnp.int32, (1, PAD), 1)
    kbias[:, 0:SEG] = jnp.where(key_mask[pl.ds(mp, 1), :] > 0, 0.0, -1e30)
    kbias[:, SEG:] = jnp.where(spare < MEM, 0.0, -1e30)

    @pl.when(mp == 0)
    def _():
        mem_recv[...] = jnp.zeros_like(mem_recv)

    @pl.when(mp == n - 1)
    def _():
        for ref in (nlow, mixed, g2low, g1low, hat2):
            ref[mem_rows, :] = jnp.zeros((PAD, width), ref.dtype)
        for j in range(parts):
            act[j, mem_rows, :] = jnp.zeros((PAD, width), BF16)
            ginner[j, mem_rows, :] = jnp.zeros((PAD, width), BF16)
        dqkv[0, mem_rows, :] = jnp.zeros((PAD, width), BF16)

    barrier = pltpu.get_barrier_semaphore()
    friends = [(dp, lax.rem(mp + step, n)) for step in range(1, n)]
    if fused:
        friends += [(lax.rem(dp + step, m), mp) for step in range(1, m)]
    for friend in friends:
        pl.semaphore_signal(barrier, inc=1, device_id=friend, device_id_type=MESH)
    pl.semaphore_wait(barrier, len(friends))

    if fused:
        events, finish_gather = gather_events(at, (ablk, up_w, down_w), fulls, gsems)
        small_copies = []
        for step in range(1, m):
            copy = remote(small_full.at[dp], small_full.at[dp], small_send.at[step - 1],
                          small_recv.at[step - 1], (lax.rem(dp + step, m), mp))
            copy.start()
            small_copies.append(copy)
        for event in events[:7]:
            event()
        for copy in small_copies:
            copy.wait()
        small[...] = jnp.concatenate([small_full[i] for i in range(m)], axis=1)
        later = list(events[7:])

        @pl.loop(0, m)
        def _(i):
            rows = pl.ds(pl.multiple_of(i * part, part), part)
            a = [afull[j, i // 4, lax.rem(i // 2, 2), lax.rem(i, 2)] for j in range(n)]
            for g in range(4):
                pieces = []
                for j in range(n):
                    pieces.append(a[j][g * part : (g + 1) * part])
                    low = (4 + g // 2) * part
                    pieces.append(a[j][low : low + part, (g % 2) * HD : (g % 2 + 1) * HD])
                row = jnp.concatenate(pieces, axis=1)
                if g < 3:
                    wqkv[g, rows, :] = row
                else:
                    wot[rows, :] = row
    else:
        small[...] = small_in[...]
        loads = [
            pltpu.make_async_copy(src, dst, w_sem.at[i])
            for i, (src, dst) in enumerate(zip(weights_hbm, (wqkv, wot, wup, wdnt)))
        ]
        for load in loads:
            load.start()
        for load in loads:
            load.wait()
        later = []
    load_cot.start()

    def onward(count):
        for event in later[:count]:
            event()
        del later[:count]

    gain1, bias1 = small[0:1], small[1:2]
    gain2, bias2 = small[2:3], small[3:4]
    lane = lax.broadcasted_iota(jnp.int32, (1, 128), 1)
    half_scaled = [
        jnp.where(lane < HD, HD**-0.5, 0.0).astype(BF16),
        jnp.where(lane < HD, 0.0, HD**-0.5).astype(BF16),
    ]
    half_one = [
        jnp.where(lane < HD, 1.0, 0.0).astype(BF16),
        jnp.where(lane < HD, 0.0, 1.0).astype(BF16),
    ]
    head_of = lax.broadcasted_iota(jnp.int32, (1, width), 1) // HD

    def head_mask(h, value):
        return jnp.where(head_of == h, value, 0.0)

    def project(rows):
        x = hid[rows, :]
        for g in range(3):
            qkv[g, rows, :] = nn(x, wqkv[g]).astype(BF16)

    def softmax(scores):
        e = jnp.exp(scores - jnp.max(scores, axis=-1, keepdims=True))
        return (e * (1.0 / jnp.sum(e, axis=-1, keepdims=True))).astype(BF16)

    lane_full = lax.broadcasted_iota(jnp.int32, (SEG, 128), 1)
    first_half = lane_full < HD
    group = 128 // PAD

    def attend_pair(pair):
        lanes = slice(pair * 128, (pair + 1) * 128)
        q = qkv[0, tok_rows, lanes]
        k = qkv[1, tok_rows, lanes]
        v = qkv[2, tok_rows, lanes]
        outs = []
        kept = stats[...]
        for half in range(2):
            h = 2 * pair + half
            scores = nt(q * half_scaled[half], k) + kbias[:, 0:SEG]
            top = jnp.max(scores, axis=-1, keepdims=True)
            e = jnp.exp(scores - top)
            kept = jnp.where(lane_full == h, top, kept)
            kept = jnp.where(lane_full == HD + h, jnp.sum(e, axis=-1, keepdims=True), kept)
            e = e.astype(BF16)
            probs[h] = e
            outs.append(nn(e, v))
        stats[...] = kept
        hat1[tok_rows, lanes] = jnp.where(first_half, outs[0], outs[1])

    def by_head(columns):
        out = columns[-1]
        for i in range(group - 1, 0, -1):
            out = jnp.where(lane_full < i * PAD, columns[i - 1], out)
        return out

    def in_head(i):
        return (lane_full >= i * PAD) & (lane_full < (i + 1) * PAD)

    def attend_to_memory():
        spread(kall, qkv[1, mem_rows, :], HD**-0.5)
        spread(vall, qkv[2, mem_rows, :], 1.0)
        scores = nt(qkv[0, tok_rows, :], kall[...])
        spare = jnp.where(lax.rem(lane_full, PAD) < MEM, 0.0, -1e30)
        for b in range(heads // group):
            lanes = slice(b * 128, (b + 1) * 128)
            part_scores = scores[:, lanes] + spare
            tops, scales, shares = [], [], []
            for i in range(group):
                h = b * group + i
                own = jnp.max(jnp.where(in_head(i), part_scores, -3e38), axis=-1, keepdims=True)
                tops.append(jnp.maximum(own, stats[:, h : h + 1]))
            e = jnp.exp(part_scores - by_head(tops))
            kept = stats[...]
            for i in range(group):
                h = b * group + i
                scale = jnp.exp(kept[:, h : h + 1] - tops[i])
                total = scale * kept[:, HD + h : HD + h + 1]
                total += jnp.sum(jnp.where(in_head(i), e, 0.0), axis=-1, keepdims=True)
                inverse = 1.0 / total
                shares.append(inverse)
                scales.append(scale * inverse)
            for i in range(group):
                kept = jnp.where(lane_full == b * group + i, scales[i], kept)
            stats[...] = kept
            pmemory[:, lanes] = (e * by_head(shares)).astype(BF16)
        extra = nn(pmemory[...], vall[...])
        for pair in range(pairs):
            lanes = slice(pair * 128, (pair + 1) * 128)
            mixed[tok_rows, lanes] = (
                hat1[tok_rows, lanes] * pair_scale(pair) + extra[:, lanes]
            ).astype(BF16)

    def pair_scale(pair):
        return jnp.where(
            first_half, stats[:, 2 * pair : 2 * pair + 1], stats[:, 2 * pair + 1 : 2 * pair + 2]
        )

    def spread(ref, x, value):
        for h in range(heads):
            ref[h * PAD : (h + 1) * PAD, :] = x * head_mask(h, value).astype(BF16)

    def gathered_heads(x):
        return sum(x[h * PAD : (h + 1) * PAD, :] * head_mask(h, 1.0) for h in range(heads))

    def attend_memory():
        spread(qall, qkv[0, mem_rows, :], HD**-0.5)
        p = softmax(nt(qall[...], qkv[1]) + kbias[...])
        pmem[...] = p
        mixed[mem_rows, :] = gathered_heads(nn(p, qkv[2])).astype(BF16)

    def each_part(rows, body):
        if rows is mem_rows:
            for j in range(parts):
                body(j)
        else:
            pl.loop(0, parts)(body)

    def feed(rows):
        resid = hid[rows, :].astype(F32) + nt(mixed[rows, :], wot[...])
        h1, i1 = normalize(resid)
        hat1[rows, :] = h1
        inv[rows, 0:1] = i1
        norm_one = h1 * gain1 + bias1
        nlow[rows, :] = norm_one.astype(BF16)
        hat2[rows, :] = norm_one

        def step(j):
            inner = nn(nlow[rows, :], wup[j])
            cumulative = 0.5 * (1.0 + lax.erf(inner * 0.7071067811865476))
            density = jnp.exp(-0.5 * inner * inner) * 0.3989422804014327
            a = (inner * cumulative).astype(BF16)
            act[j, rows, :] = a
            slope[j, rows, :] = (cumulative + inner * density).astype(BF16)
            hat2[rows, :] += nt(a, wdnt[j])

        each_part(rows, step)
        h2, i2 = normalize(hat2[rows, :])
        hat2[rows, :] = h2
        inv[rows, 1:2] = i2
        return (h2 * gain2 + bias2).astype(BF16)

    def feed_back(rows, grad_final):
        h2 = hat2[rows, :]
        dnorm[2:3, :] += jnp.sum(grad_final * h2, axis=0, keepdims=True)
        dnorm[3:4, :] += jnp.sum(grad_final, axis=0, keepdims=True)
        g2 = normalize_back(grad_final, h2, inv[rows, 1:2], gain2)
        g2low[rows, :] = g2.astype(BF16)
        gone[rows, :] = g2

        def step(j):
            gi = (nn(g2low[rows, :], wdnt[j]) * slope[j, rows, :].astype(F32)).astype(BF16)
            ginner[j, rows, :] = gi
            gone[rows, :] += nt(gi, wup[j])

        each_part(rows, step)
        grad_norm = gone[rows, :]
        h1 = hat1[rows, :]
        dnorm[0:1, :] += jnp.sum(grad_norm * h1, axis=0, keepdims=True)
        dnorm[1:2, :] += jnp.sum(grad_norm, axis=0, keepdims=True)
        g1 = normalize_back(grad_norm, h1, inv[rows, 0:1], gain1)
        gone[rows, :] = g1
        low = g1.astype(BF16)
        g1low[rows, :] = low
        gmix[rows, :] = nn(low, wot[...]).astype(BF16)

    def memory_keys_back():
        dprob = nt(gmix[tok_rows, :], vall[...])
        deltas = []
        for pair in range(pairs):
            lanes = slice(pair * 128, (pair + 1) * 128)
            product = gmix[tok_rows, lanes].astype(F32) * mixed[tok_rows, lanes].astype(F32)
            deltas.append(jnp.sum(jnp.where(first_half, product, 0.0), axis=-1, keepdims=True))
            deltas.append(jnp.sum(jnp.where(first_half, 0.0, product), axis=-1, keepdims=True))
        grads = []
        for b in range(heads // group):
            lanes = slice(b * 128, (b + 1) * 128)
            delta = by_head(deltas[b * group : (b + 1) * group])
            grads.append(
                (pmemory[:, lanes].astype(F32) * (dprob[:, lanes] - delta)).astype(BF16)
            )
        ds = jnp.concatenate(grads, axis=1)
        dqkv[0, tok_rows, :] = nn(ds, kall[...]).astype(BF16)
        dk = gathered_heads(tn(ds, qkv[0, tok_rows, :])) * HD**-0.5
        dqkv[1, mem_rows, :] = dk.astype(BF16)
        dqkv[2, mem_rows, :] = gathered_heads(tn(pmemory[...], gmix[tok_rows, :])).astype(BF16)

    def attend_back():
        for pair in range(pairs):
            lanes = slice(pair * 128, (pair + 1) * 128)
            scaled = gmix[tok_rows, lanes].astype(F32) * pair_scale(pair)
            gmix[tok_rows, lanes] = scaled.astype(BF16)

        @pl.loop(0, pairs)
        def _(pair):
            lanes = pl.ds(pl.multiple_of(pair * 128, 128), 128)
            q = qkv[0, tok_rows, lanes]
            k = qkv[1, tok_rows, lanes]
            v = qkv[2, tok_rows, lanes]
            g = gmix[tok_rows, lanes]
            product = g.astype(F32) * mixed[tok_rows, lanes].astype(F32)
            dqs = []
            dk = None
            dv = None
            for half in range(2):
                e = probs[2 * pair + half]
                gh = g * half_one[half]
                inside = first_half if half == 0 else ~first_half
                delta = jnp.sum(jnp.where(inside, product, 0.0), axis=-1, keepdims=True)
                ds = (e.astype(F32) * (nt(gh, v) - delta)).astype(BF16)
                dv_h = tn(e, gh)
                dk_h = tn(ds, q * half_scaled[half])
                dqs.append(nn(ds, k))
                dk = dk_h if dk is None else dk + dk_h
                dv = dv_h if dv is None else dv + dv_h
            dq = jnp.where(first_half, dqs[0], dqs[1]) * HD**-0.5
            dq += dqkv[0, tok_rows, lanes].astype(F32)
            dqkv[0, tok_rows, lanes] = dq.astype(BF16)
            dqkv[1, tok_rows, lanes] = dk.astype(BF16)
            dqkv[2, tok_rows, lanes] = dv.astype(BF16)

    def more(g, rows, extra):
        dqkv[g, rows, :] = (dqkv[g, rows, :].astype(F32) + extra).astype(BF16)

    def attend_back_memory():
        spread(qall, qkv[0, mem_rows, :], HD**-0.5)
        spread(gall, gmix[mem_rows, :], 1.0)
        dprob = nt(gall[...], qkv[2])
        pf = pmem[...].astype(F32)
        delta = jnp.sum(pf * dprob, axis=-1, keepdims=True)
        ds = (pf * (dprob - delta)).astype(BF16)
        dqkv[0, mem_rows, :] = (gathered_heads(nn(ds, qkv[1])) * HD**-0.5).astype(BF16)
        more(1, mem_rows, tn(ds[:, SEG:], qall[...]))
        more(2, mem_rows, tn(pmem[:, SEG:], gall[...]))
        probs[0, 0 : heads * PAD, :] = ds[:, 0:SEG]

    def attend_back_tokens():
        more(1, tok_rows, tn(probs[0, 0 : heads * PAD, :], qall[...]))
        more(2, tok_rows, tn(pmem[:, 0:SEG], gall[...]))

    def chain_copy(src, dst, slot, peer):
        return remote(src, dst, chain_sem.at[2 * slot], chain_sem.at[2 * slot + 1], (dp, peer))

    forward_copy = chain_copy(mem_send, mem_recv, 0, lax.rem(mp + 1, n))
    backward_copy = chain_copy(gm_send, gm_recv, 1, lax.rem(mp + n - 1, n))

    def take_memory():
        memory = small[4 : 4 + MEM, :]
        memory = jnp.concatenate([memory, jnp.zeros((PAD - MEM, width), F32)], axis=0)
        memory = jnp.where(starts, memory, mem_recv[...].astype(F32))
        hid[mem_rows, :] = memory.astype(BF16)
        project(mem_rows)

    load_tok.wait()
    onward(1)
    for c in range(2):
        project(pl.ds(c * 256, 256))
        onward(1)
    stats[...] = jnp.zeros_like(stats)
    for pair in range(pairs):
        attend_pair(pair)
        if pair == 3:

            @pl.when(mp == 0)
            def _():
                take_memory()
                attend_memory()

        if pair % 2 == 0:
            onward(1)
    onward(len(later))

    @pl.when(mp > 0)
    def _():
        forward_copy.wait_recv()
        take_memory()

    @pl.when((mp > 0) & (mp < n - 1))
    def _():
        attend_memory()

    @pl.when(mp < n - 1)
    def _():
        mem_send[...] = feed(mem_rows)
        forward_copy.start()

    attend_to_memory()

    @pl.loop(0, 2)
    def _(c):
        rows = pl.ds(pl.multiple_of(c * 256, 256), 256)
        lout[rows, :] = feed(rows)

    own = pl.ds(mp * SEG, SEG)
    keep_out = pltpu.make_async_copy(lout.at[tok_rows], lo_hbm.at[own], lo_sem)
    keep_out.start()
    keep_out.wait()
    out_copies = []
    size = SEG // PIECES

    def send_out(first, last):
        for piece in range(first, last):
            for step in (3, 2, 1):
                rows = pl.ds(mp * SEG + piece * size, size)
                copy = remote(lo_hbm.at[rows], lo_hbm.at[rows], lo_send.at[piece, step - 1],
                              lo_recv.at[piece, step - 1], (dp, at["z"][step]))
                copy.start()
                out_copies.append(copy)

    send_out(0, 3)

    dnorm[...] = jnp.zeros_like(dnorm)
    load_cot.wait()

    @pl.loop(0, 2)
    def _(c):
        rows = pl.ds(pl.multiple_of(c * 256, 256), 256)
        feed_back(rows, cot[rows, :].astype(F32))

    def input_grad(rows):
        return (
            gone[rows, :]
            + nt(dqkv[0, rows, :], wqkv[0])
            + nt(dqkv[1, rows, :], wqkv[1])
            + nt(dqkv[2, rows, :], wqkv[2])
        )

    def give_memory_grad():
        gmem = input_grad(mem_rows)
        gm_send[...] = jnp.where(carries, gmem, 0.0).astype(BF16)

        @pl.when(mp > 0)
        def _():
            backward_copy.start()

        dmem[...] = jnp.where(starts, gmem, 0.0)

    memory_keys_back()

    @pl.when(mp == n - 1)
    def _():
        give_memory_grad()

    attend_back()

    @pl.when(mp < n - 1)
    def _():
        backward_copy.wait_recv()
        feed_back(mem_rows, gm_recv[...].astype(F32))
        attend_back_memory()
        give_memory_grad()

    send_out(3, 4)
    cols = width // n
    for i in range(m):
        tiny[i, 0:MEM, :] = dmem[0:MEM, i * part : (i + 1) * part]
        tiny[i, MEM:, :] = dnorm[0:4, i * part : (i + 1) * part]
    dx_copies = []

    def tokens_back():
        @pl.when(mp < n - 1)
        def _():
            attend_back_tokens()

        for c in range(2):
            rows = pl.ds(c * 256, 256)
            g = gone[rows, :].T
            for j in range(3):
                g += nt(wqkv[j], dqkv[j, rows, :])
            g = g.astype(BF16)
            for j in range(n):
                dxs[j, :, rows] = g[j * cols : (j + 1) * cols]

        keep_dx = pltpu.make_async_copy(dxs.at[mp], dx_hbm.at[mp], dx_sem)
        keep_dx.start()
        dx_copies.append(keep_dx)
        for step in range(1, n):
            peer = at['z'][step]
            copy = remote(dxs.at[peer], dx_hbm.at[mp], dx_send.at[step - 1],
                          dx_recv.at[step - 1], (dp, peer))
            copy.start()
            dx_copies.append(copy)

    def in_thirds(body):
        @pl.loop(0, width // 256)
        def _(i):
            body(pl.ds(pl.multiple_of(i * 256, 256), 256))

    def down_grad(j):
        def third(some):
            wdnt[j, some, :] = tn(g2low[:, some], act[j]).astype(BF16)

        in_thirds(third)

    def up_grad(j):
        def third(some):
            wup[j, some, :] = tn(nlow[:, some], ginner[j]).astype(BF16)

        in_thirds(third)

    def attend_grads():
        def third(some):
            wot[some, :] = tn(g1low[:, some], mixed[...]).astype(BF16)
            for g in range(3):
                wqkv[g, some, :] = tn(hid[:, some], dqkv[g]).astype(BF16)

        in_thirds(third)

    if fused:
        finish_gather()
        tiny_start, tiny_end = tiny_steps(at, tiny, tsum, trecv, t_send, t_recv)
        f1, fetch, f2, f3, f4, total_of, finish_scatter = scatter_steps(
            at, (dfull, ufull, afull), firsts, rings, r2x, r2y, r3x, r3y, r4, ssems
        )
        tiny_start(0)
        order = (3, 2, 1, 0)
        for s in range(15):
            if s < 4:
                down_grad(at["z"][order[s]])
            elif s < 8:
                up_grad(at["z"][order[s - 4]])
            elif s == 8:
                tokens_back()
                attend_grads()

                @pl.loop(0, m)
                def _(i):
                    rows = pl.ds(pl.multiple_of(i * part, part), part)
                    w = [wqkv[g, rows, :] if g < 3 else wot[rows, :] for g in range(4)]
                    for j in range(n):
                        lo = j * cols
                        spot = afull.at[j, i // 4, lax.rem(i // 2, 2), lax.rem(i, 2)]
                        for g in range(4):
                            spot[g * part : (g + 1) * part, :] = w[g][:, lo : lo + 128]
                        for g in range(2):
                            spot[(4 + g) * part : (5 + g) * part, :] = jnp.concatenate(
                                [w[2 * g][:, lo + 128 : lo + cols],
                                 w[2 * g + 1][:, lo + 128 : lo + cols]],
                                axis=1,
                            )

            if s in (0, 2, 4, 6):
                send_out(s // 2 + 4, s // 2 + 5)
            if s < 12:
                f1(s)
            if 1 <= s < 13:
                fetch(s - 1)
            if 2 <= s < 14:
                f3(s - 2)
            if 3 <= s:
                f4(s - 3)
            if 1 <= s < 13:
                f2(s - 1)
            if s < 5:
                tiny_end(s)
                if s < 4:
                    tiny_start(s + 1)
        done = tsum[0, dp]
        dmem_out[...] = done[0:MEM]
        for i in range(4):
            dnorm_out[i][...] = done[MEM + i : MEM + i + 1]
        ddown_out[...] = total_of(0)
        dup_out[...] = total_of(1)
        a = total_of(2)
        for g in range(4):
            edge = a[(4 + g // 2) * part : (5 + g // 2) * part, (g % 2) * HD : (g % 2 + 1) * HD]
            block = jnp.concatenate([a[g * part : (g + 1) * part], edge], axis=1)
            if g < 3:
                dqkv_out[g] = block
            else:
                dout_out[...] = block.T
        finish_scatter()
    else:
        send_out(4, PIECES)
        tokens_back()
        pl.loop(0, parts)(down_grad)
        pl.loop(0, parts)(up_grad)
        attend_grads()
        stores = [
            pltpu.make_async_copy(src, dst, w_sem.at[i])
            for i, (src, dst) in enumerate(zip((wqkv, wot, wup, wdnt), grads_hbm))
        ]
        for store in stores:
            store.start()
        for store in stores:
            store.wait()
    for copy in out_copies + dx_copies:
        copy.wait()

    @pl.when(mp < n - 1)
    def _():
        forward_copy.wait_send()

    @pl.when(mp > 0)
    def _():
        backward_copy.wait_send()


def run_layer(n, m, fused, tokens, cotangent, resets, truncation, key_mask, *rest):
    width = tokens.shape[1]
    parts = n
    heads = width // HD
    part = width // m
    vmem = pl.BlockSpec(memory_space=pltpu.VMEM)
    smem = pl.BlockSpec(memory_space=pltpu.SMEM)
    anyspace = pl.BlockSpec(memory_space=pl.ANY)
    sems = pltpu.SemaphoreType.DMA
    out_shape = [
        jax.ShapeDtypeStruct((n * SEG, width), BF16),
        jax.ShapeDtypeStruct((n, width // n, SEG), BF16),
    ]
    if fused:
        pieces = [(6 * part, 128), (part, width), (part, width)]
        backward = [pieces[2], pieces[1], pieces[0]]
        out_shape += [jax.ShapeDtypeStruct((4, 2, 2) + p, BF16) for p in backward]
        out_shape += [jax.ShapeDtypeStruct(w.shape, F32) for w in rest[5:]]
        out_shape += [jax.ShapeDtypeStruct((MEM, part), F32)]
        out_shape += [jax.ShapeDtypeStruct((1, part), F32)] * 4
        in_rest = [vmem] * len(rest)
        out_specs = [anyspace] * 5 + [vmem] * 9
        first = (
            [pltpu.VMEM((m, 32, part), F32), pltpu.VMEM((32, part), F32),
             pltpu.VMEM(pieces[0], BF16)]
            + [pltpu.VMEM((4, 2, 2, 2) + p, BF16) for p in pieces]
            + gather_sems(3)
            + [sems((m - 1,)), sems((m - 1,))]
            + [pltpu.VMEM((3, width, width), BF16), pltpu.VMEM((width, width), BF16)]
            + [pltpu.VMEM((2, 2) + pieces[0], BF16)]
            + scatter_scratch(backward)
            + [pltpu.VMEM((m, MEM + 4, part), F32), pltpu.VMEM((2, m, MEM + 4, part), F32),
               pltpu.VMEM((5, m, MEM + 4, part), F32), sems((5,)), sems((5,))]
        )
    else:
        shapes = [w.shape for w in rest[1:]]
        out_shape += [jax.ShapeDtypeStruct(s, BF16) for s in shapes]
        out_shape += [jax.ShapeDtypeStruct((m, MEM + 4, part), F32)]
        in_rest = [vmem] + [anyspace] * 4
        out_specs = [anyspace] * 6 + [vmem]
        first = [pltpu.VMEM(s, BF16) for s in shapes]
    row_bf = pltpu.VMEM((ROWS, width), BF16)
    row_f = pltpu.VMEM((ROWS, width), F32)
    one_f = pltpu.VMEM((ROWS, 2), F32)
    wide = pltpu.VMEM((parts, ROWS, width), BF16)
    mem_bf = pltpu.VMEM((PAD, width), BF16)
    all_bf = pltpu.VMEM((heads * PAD, width), BF16)
    return pl.pallas_call(
        functools.partial(layer_kernel, n, m, fused),
        out_shape=tuple(out_shape),
        in_specs=[anyspace, anyspace, smem, smem, vmem] + in_rest,
        out_specs=tuple(out_specs),
        scratch_shapes=first + [
            pltpu.VMEM((1, ROWS), F32), pltpu.VMEM((32, width), F32),
            pltpu.VMEM((heads * PAD, ROWS), BF16), all_bf, all_bf,
            pltpu.VMEM((SEG, heads * PAD), BF16), pltpu.VMEM((SEG, 128), F32),
            row_bf, pltpu.VMEM((SEG, width), BF16), pltpu.VMEM((3, ROWS, width), BF16),
            pltpu.VMEM((heads, SEG, SEG), BF16), row_bf, row_f, one_f, row_bf, wide, wide, row_f,
            row_bf, row_bf, row_bf, pltpu.VMEM((3, ROWS, width), BF16),
            pltpu.VMEM((n, width // n, SEG), BF16),
            pltpu.VMEM((8, width), F32), pltpu.VMEM((PAD, width), F32),
            mem_bf, mem_bf, mem_bf, mem_bf,
            sems((2,)), sems((4,)), sems, sems, sems((PIECES, n - 1)), sems((PIECES, n - 1)), sems((n - 1,)),
            sems((n - 1,)), sems((4,)),
        ],
        compiler_params=pltpu.CompilerParams(
            collective_id=0, has_side_effects=True, vmem_limit_bytes=255 * 2**18
        ),
        cost_estimate=pl.CostEstimate(
            flops=26_000_000_000, bytes_accessed=40_000_000, transcendentals=10_000_000
        ),
    )(tokens, cotangent, resets, truncation, key_mask, *rest)


def finish_kernel(lo_in, dx_in, *refs):
    count = (len(refs) - 5) // 2
    lo_out, dx_out, held, sem_in, sem_out = refs[count], refs[count + 1], *refs[-3:]
    pieces, size = held.shape[:2]
    loads = [
        pltpu.make_async_copy(lo_in.at[pl.ds(i * size, size)], held.at[i], sem_in.at[i])
        for i in range(pieces)
    ]
    stores = [
        pltpu.make_async_copy(held.at[i], lo_out.at[pl.ds(i * size, size)], sem_out.at[i])
        for i in range(pieces)
    ]
    for load in loads:
        load.start()
    for j in range(dx_in.shape[0]):
        dx_out[:, j * SEG : (j + 1) * SEG] = dx_in[j].astype(F32)
    for src, dst in zip(refs[:count], refs[count + 2 : -3]):
        dst[...] = src[...]
    for load, store in zip(loads, stores):
        load.wait()
        store.start()
    for store in stores:
        store.wait()


def finish_outputs(lo, dx, *rest):
    vmem = pl.BlockSpec(memory_space=pltpu.VMEM)
    anyspace = pl.BlockSpec(memory_space=pl.ANY)
    n, cols, rows = dx.shape
    return pl.pallas_call(
        finish_kernel,
        out_shape=(
            jax.ShapeDtypeStruct(lo.shape, lo.dtype),
            jax.ShapeDtypeStruct((cols, n * rows), F32),
            *[jax.ShapeDtypeStruct(r.shape, r.dtype) for r in rest],
        ),
        in_specs=[anyspace] + [vmem] * (1 + len(rest)),
        out_specs=(anyspace,) + (vmem,) * (1 + len(rest)),
        scratch_shapes=[
            pltpu.VMEM((n, lo.shape[0] // n, lo.shape[1]), BF16),
            pltpu.SemaphoreType.DMA((n,)),
            pltpu.SemaphoreType.DMA((n,)),
        ],
        compiler_params=pltpu.CompilerParams(vmem_limit_bytes=60 * 2**20),
    )(lo, dx, *rest)


def shards(
    tokens, cotangent, resets, key_mask, truncation_segments, qkv_weight, out_weight, up_weight,
    down_weight, memory_init, norm1_gain, first_norm_bias, norm2_gain, norm2_bias,
):
    n = lax.axis_size("mp")
    m = lax.axis_size("dp")
    width = tokens.shape[1]
    slots = resets.shape[0]
    rows = width // m
    cols = width // n
    if m == 8 and n == 4 and width == 768:
        out = run_layer(
            n, m, True, tokens, cotangent, resets, truncation_segments,
            key_mask.reshape(slots, SEG), norm1_gain[None], first_norm_bias[None],
            norm2_gain[None], norm2_bias[None], memory_init, qkv_weight, out_weight, up_weight,
            down_weight.T,
        )
        lo, dx, *rest = finish_outputs(*out[:2], *out[5:])
        return (lo, dx.T, *rest[:3], rest[3].T, rest[4], *[d[0] for d in rest[5:]])
    small = jnp.concatenate(
        [norm1_gain[None], first_norm_bias[None], norm2_gain[None], norm2_bias[None], memory_init,
         jnp.zeros((32 - 4 - MEM, rows), BF16)],
        axis=0,
    )
    block = jnp.concatenate([qkv_weight, out_weight.T[None]], axis=0)
    block = lax.all_gather(block, ("mp", "dp"), axis=0)
    block = block.reshape(n, m, 4, rows, cols).transpose(2, 1, 3, 0, 4).reshape(4, width, width)
    wup = lax.all_gather(up_weight, ("mp", "dp"), axis=0).reshape(n, width, -1)
    wdnt = lax.all_gather(down_weight.T, ("mp", "dp"), axis=0).reshape(n, width, -1)
    small = lax.all_gather(small, "dp", axis=1, tiled=True).astype(F32)
    lo, dx, dqkv, dot_w, dup, ddnt, tiny = run_layer(
        n, m, False, tokens, cotangent, resets, truncation_segments, key_mask.reshape(slots, SEG),
        small, block[:3], block[3], wup, wdnt,
    )
    dblock = jnp.concatenate([dqkv, dot_w[None]], axis=0)
    dblock = dblock.reshape(4, m, rows, n, cols).transpose(3, 1, 0, 2, 4)
    dblock = dblock.reshape(n * m, 4, rows, cols)
    dblock = lax.psum_scatter(dblock, ("mp", "dp"), scatter_dimension=0).astype(F32)
    dup = lax.psum_scatter(
        dup.reshape(n * m, rows, -1), ("mp", "dp"), scatter_dimension=0
    ).astype(F32)
    ddnt = lax.psum_scatter(
        ddnt.reshape(n * m, rows, -1), ("mp", "dp"), scatter_dimension=0
    ).astype(F32)
    tiny = lax.psum(tiny, ("mp", "dp"))[lax.axis_index("dp")]
    return (
        lo,
        dx.astype(F32).transpose(0, 2, 1).reshape(n * SEG, cols),
        dblock[:3],
        dblock[3].T,
        dup,
        ddnt.T,
        tiny[:MEM],
        tiny[MEM],
        tiny[MEM + 1],
        tiny[MEM + 2],
        tiny[MEM + 3],
    )


def solution(mesh):
    return jax.shard_map(
        shards,
        mesh=mesh,
        in_specs=(
            P("dp", None), P("dp", None), P("dp"), P("dp"), P(),
            P(None, "dp", "mp"), P("mp", "dp"), P("dp", "mp"), P("mp", "dp"), P(None, "dp"),
            P("dp"), P("dp"), P("dp"), P("dp"),
        ),
        out_specs=(
            P("dp", None), P("dp", "mp"), P(None, "dp", "mp"), P("mp", "dp"), P("dp", "mp"),
            P("mp", "dp"), P(None, "dp"), P("dp"), P("dp"), P("dp"), P("dp"),
        ),
        check_vma=False,
    )
```

```python
import functools

import jax
import jax.numpy as jnp
from jax import lax
from jax.experimental import pallas as pl
from jax.experimental.pallas import tpu as pltpu
from jax.sharding import PartitionSpec as P

HD = 64
SEG = 512
MEM = 20
PAD = 32
ROWS = SEG + PAD
PIECES = 8
EPSILON = 1e-05
MESH = pl.DeviceIdType.MESH
F32 = jnp.float32
BF16 = jnp.bfloat16


def nn(a, b):
    return lax.dot_general(a, b, (((1,), (0,)), ((), ())), preferred_element_type=F32)


def nt(a, b):
    return lax.dot_general(a, b, (((1,), (1,)), ((), ())), preferred_element_type=F32)


def tn(a, b):
    return lax.dot_general(a, b, (((0,), (0,)), ((), ())), preferred_element_type=F32)


def normalize(resid):
    center = resid - jnp.mean(resid, axis=-1, keepdims=True)
    inverse = lax.rsqrt(jnp.mean(center * center, axis=-1, keepdims=True) + EPSILON)
    return center * inverse, inverse


def normalize_back(grad_out, hat, inverse, gain):
    grad_hat = grad_out * gain
    return inverse * (
        grad_hat
        - jnp.mean(grad_hat, axis=-1, keepdims=True)
        - hat * jnp.mean(grad_hat * hat, axis=-1, keepdims=True)
    )


def place(n):
    dp = lax.axis_index("dp")
    mp = lax.axis_index("mp")
    c, x, y = lax.rem(dp, 2), lax.rem(dp // 2, 2), dp // 4
    return {
        "c": c,
        "x": x,
        "y": y,
        "mp": mp,
        "core": (dp + 1 - 2 * c, mp),
        "xp": (dp + 2 - 4 * x, mp),
        "yp": (dp + 4 - 8 * y, mp),
        "z": [mp, mp + 1 - 2 * lax.rem(mp, 2), lax.rem(mp + 2, 4), 3 - mp],
        "dp": dp,
    }


def remote(src, dst, send, recv, peer):
    return pltpu.make_async_remote_copy(
        src_ref=src, dst_ref=dst, send_sem=send, recv_sem=recv, device_id=peer, device_id_type=MESH
    )


def gather_events(at, shards_in, fulls, sems):
    z_send, z_recv, s1_send, s1_recv, s2_send, s2_recv, c_send, c_recv, own_sem = sems
    c, x, y, mp = at["c"], at["x"], at["y"], at["mp"]
    mine, by_x, by_y, diag = (y, x), (y, 1 - x), (1 - y, x), (1 - y, 1 - x)
    kinds = len(shards_in)
    sent = []
    own = []

    def go(copy):
        copy.start()
        sent.append(copy)
        return copy

    def arrived(ref, sem):
        remote(ref, ref, s1_send.at[0, 0], sem, at["core"]).wait_recv()

    def start_z(t):
        for k in range(1, 4):
            go(remote(shards_in[t], fulls[t].at[mp, *mine, c], z_send.at[t, k - 1],
                      z_recv.at[t, k - 1], (at["dp"], at["z"][k])))

    def e1(t, k):
        s = 4 * t + k
        j = at["z"][k]
        full = fulls[t]
        piece = full.at[j, *mine, c]
        if k == 0:
            keep = pltpu.make_async_copy(shards_in[t], piece, own_sem.at[t])
            keep.start()
            own.append(keep)
            src = shards_in[t]
        else:
            arrived(piece, z_recv.at[t, k - 1])
            src = piece
        go(remote(src, piece, s1_send.at[s, 0], s1_recv.at[s, 0], at["xp"]))
        go(remote(src, piece, s1_send.at[s, 1], s1_recv.at[s, 1], at["yp"]))
        go(remote(src, piece, c_send.at[s, 0], c_recv.at[s, 0], at["core"]))

    def e2(t, k):
        s = 4 * t + k
        full = fulls[t]
        j = at["z"][k]
        half = full.shape[4] // 2
        px, py = full.at[j, *by_x, c], full.at[j, *by_y, c]
        arrived(px, s1_recv.at[s, 0])
        low = full.at[j, *by_x, c, pl.ds(0, half)]
        go(remote(low, low, s2_send.at[s, 1], s2_recv.at[s, 1], at["yp"]))
        go(remote(px, px, c_send.at[s, 1], c_recv.at[s, 1], at["core"]))
        arrived(py, s1_recv.at[s, 1])
        high = full.at[j, *by_y, c, pl.ds(half, half)]
        go(remote(high, high, s2_send.at[s, 0], s2_recv.at[s, 0], at["xp"]))
        go(remote(py, py, c_send.at[s, 2], c_recv.at[s, 2], at["core"]))

    def e3(t, k):
        s = 4 * t + k
        full = fulls[t]
        j = at["z"][k]
        half = full.shape[4] // 2
        arrived(full.at[j, *diag, c, pl.ds(half, half)], s2_recv.at[s, 0])
        arrived(full.at[j, *diag, c, pl.ds(0, half)], s2_recv.at[s, 1])
        pd = full.at[j, *diag, c]
        go(remote(pd, pd, c_send.at[s, 3], c_recv.at[s, 3], at["core"]))

    def e4(t, k):
        s = 4 * t + k
        full = fulls[t]
        j = at["z"][k]
        for q, spot in enumerate((mine, by_x, by_y, diag)):
            arrived(full.at[j, *spot, 1 - c], c_recv.at[s, q])
        if k == 0:
            own[t].wait()

    events = []
    order = [(t, k) for t in range(kinds) for k in range(4)]
    total = len(order)
    for s in range(total + 3):
        def event(s=s):
            if s == 0:
                start_z(0)
            if s % 4 == 1 and s // 4 + 1 < kinds:
                start_z(s // 4 + 1)
            if s < total:
                e1(*order[s])
            if 0 <= s - 1 < total:
                e2(*order[s - 1])
            if 0 <= s - 2 < total:
                e3(*order[s - 2])
            if 0 <= s - 3 < total:
                e4(*order[s - 3])
        events.append(event)

    def finish():
        for copy in sent:
            copy.wait_send()

    return events, finish


def gather_sems(kinds):
    sems = pltpu.SemaphoreType.DMA
    total = 4 * kinds
    return [
        sems((kinds, 3)), sems((kinds, 3)), sems((total, 2)), sems((total, 2)), sems((total, 2)),
        sems((total, 2)), sems((total, 4)), sems((total, 4)), sems((kinds,)),
    ]


def scatter_steps(at, fulls, firsts, rings, r2x, r2y, r3x, r3y, r4, sems):
    c_send, c_recv, l_sem, s1_send, s1_recv, s2_send, s2_recv, z_send, z_recv = sems
    c, x, y = at["c"], at["x"], at["y"]
    order = (3, 2, 1, 0)
    sent = []

    def go(copy):
        copy.start()
        sent.append(copy)

    def arrived(ref, sem):
        remote(ref, ref, c_send.at[0], sem, at["core"]).wait_recv()

    def spot(s):
        t, q = s // 4, s % 4
        return t, q, at["z"][order[q]], fulls[t].shape[4] // 2

    def load(s):
        t, q, _, _ = spot(s)
        return pltpu.make_async_copy(firsts[t].at[q], rings[t], l_sem.at[s])

    def f1(s):
        t, q, j, _ = spot(s)
        go(remote(fulls[t].at[j, :, :, 1 - c], firsts[t].at[q], c_send.at[s], c_recv.at[s],
                  at["core"]))

    def fetch(s):
        t, q, _, _ = spot(s)
        arrived(firsts[t].at[q], c_recv.at[s])
        load(s).start()

    def add(p, q):
        return (p.astype(F32) + q.astype(F32)).astype(BF16)

    def f2(s):
        t, q, j, half = spot(s)
        full = fulls[t]
        load(s).wait()
        for yy in range(2):
            for xx in range(2):
                full[j, yy, xx, c] = add(full[j, yy, xx, c], rings[t][yy, xx])
        go(remote(full.at[j, :, 1 - x, c, pl.ds(0, half)], r2x[t].at[q],
                  s1_send.at[s, 0], s1_recv.at[s, 0], at["xp"]))
        go(remote(full.at[j, 1 - y, :, c, pl.ds(half, half)], r2y[t].at[q],
                  s1_send.at[s, 1], s1_recv.at[s, 1], at["yp"]))

    def f3(s):
        t, q, j, half = spot(s)
        full = fulls[t]
        low, high = slice(0, half), slice(half, 2 * half)
        arrived(r2x[t].at[q], s1_recv.at[s, 0])
        for v in range(2):
            full[j, v, x, c, low] = add(full[j, v, x, c, low], r2x[t][q, v])
        go(remote(full.at[j, 1 - y, x, c, pl.ds(0, half)], r3y[t].at[q],
                  s2_send.at[s, 1], s2_recv.at[s, 1], at["yp"]))
        arrived(r2y[t].at[q], s1_recv.at[s, 1])
        for v in range(2):
            full[j, y, v, c, high] = add(full[j, y, v, c, high], r2y[t][q, v])
        go(remote(full.at[j, y, 1 - x, c, pl.ds(half, half)], r3x[t].at[q],
                  s2_send.at[s, 0], s2_recv.at[s, 0], at["xp"]))

    def f4(s):
        t, q, j, half = spot(s)
        full = fulls[t]
        k = order[q]
        low, high = slice(0, half), slice(half, 2 * half)
        arrived(r3y[t].at[q], s2_recv.at[s, 1])
        arrived(r3x[t].at[q], s2_recv.at[s, 0])
        full[j, y, x, c, low] = add(full[j, y, x, c, low], r3y[t][q])
        full[j, y, x, c, high] = add(full[j, y, x, c, high], r3x[t][q])
        if k:
            go(remote(full.at[j, y, x, c], r4[t].at[k - 1], z_send.at[t, k - 1],
                      z_recv.at[t, k - 1], (at["dp"], at["z"][k])))

    def total_of(t):
        got = fulls[t][at["mp"], y, x, c].astype(F32)
        for k in range(1, 4):
            arrived(r4[t].at[k - 1], z_recv.at[t, k - 1])
            got += r4[t][k - 1].astype(F32)
        return got

    def finish():
        for copy in sent:
            copy.wait_send()

    return f1, fetch, f2, f3, f4, total_of, finish


def scatter_scratch(shapes):
    sems = pltpu.SemaphoreType.DMA
    kinds = len(shapes)
    total = 4 * kinds

    def per(f):
        return [pltpu.VMEM(f(r, w), BF16) for r, w in shapes]

    return (
        per(lambda r, w: (4, 2, r // 2, w))
        + per(lambda r, w: (4, 2, r // 2, w))
        + per(lambda r, w: (4, r // 2, w))
        + per(lambda r, w: (4, r // 2, w))
        + per(lambda r, w: (3, r, w))
        + [sems((total,)), sems((total,)), sems((total,)), sems((total, 2)), sems((total, 2)),
           sems((total, 2)), sems((total, 2)), sems((kinds, 3)), sems((kinds, 3))]
    )


def tiny_steps(at, tiny, tsum, trecv, t_send, t_recv):
    peers = [at["core"], at["xp"], at["yp"], (at["dp"], at["z"][1]), (at["dp"], at["z"][2])]

    def copy(q):
        src = tiny if q == 0 else tsum.at[(q - 1) % 2]
        return remote(src, trecv.at[q], t_send.at[q], t_recv.at[q], peers[q])

    def end(q):
        copy(q).wait()
        tsum[q % 2] = (tiny[...] if q == 0 else tsum[(q - 1) % 2]) + trecv[q]

    return (lambda q: copy(q).start()), end


def layer_kernel(n, m, fused, *refs):
    at = place(n)
    dp, mp = lax.axis_index("dp"), lax.axis_index("mp")
    take = iter(refs)

    def some(count):
        return [next(take) for _ in range(count)]

    tok_hbm, cot_hbm, resets, truncation, key_mask = some(5)
    if fused:
        norm_in, (memory_in, qkv_w, out_w, up_w, down_w) = some(4), some(5)
        lo_hbm, dx_hbm = some(2)
        firsts = some(3)
        dqkv_out, dout_out, dup_out, ddown_out, dmem_out, *dnorm_out = some(9)
        small_full, small_own, ablk = some(3)
        fulls = some(3)
        gsems = some(9)
        small_send, small_recv = some(2)
        wqkv, wot, ring_a = some(3)
        r2x, r2y, r3x, r3y, r4 = [some(3) for _ in range(5)]
        ssems = some(9)
        tiny, tsum, trecv, t_send, t_recv = some(5)
        afull, ufull, dfull = fulls
        parts = n
        width = wot.shape[0]
        wup = ufull.reshape(n, width, width)
        wdnt = dfull.reshape(n, width, width)
    else:
        small_in, weights_hbm = next(take), some(4)
        lo_hbm, dx_hbm = some(2)
        grads_hbm, tiny = some(4), next(take)
        wqkv, wot, wup, wdnt = some(4)
    (
        kbias, small, pmem, kall, vall, pmemory, stats,
        hid, cot, qkv, probs, mixed, hat1, inv, nlow, act, slope, hat2,
        g2low, g1low, gmix, dqkv, dxs, dnorm, dmem,
        mem_recv, mem_send, gm_recv, gm_send,
        load_sem, w_sem, lo_sem, dx_sem, lo_send, lo_recv, dx_send, dx_recv, chain_sem,
    ) = some(38)
    qall, gall = kall, vall
    ginner, gone, lout = slope, hat2, gmix
    if fused:
        ring_b = cot.at[pl.ds(0, 4 * up_w.shape[0])].reshape(2, 2, *up_w.shape)
        rings = (ring_b, ring_b, ring_a)
    width = hid.shape[1]
    heads = width // HD
    pairs = width // 128
    parts = n
    part = width // m
    tok_rows = pl.ds(0, SEG)
    mem_rows = pl.ds(SEG, PAD)

    load_tok = pltpu.make_async_copy(
        tok_hbm.at[pl.ds(mp * SEG, SEG)], hid.at[tok_rows], load_sem.at[0]
    )
    load_cot = pltpu.make_async_copy(cot_hbm.at[pl.ds(mp * SEG, SEG)], cot, load_sem.at[1])
    load_tok.start()
    if fused:
        for i, ref in enumerate(norm_in):
            small_own[i : i + 1, :] = ref[...].astype(F32)
        small_own[4 : 4 + MEM, :] = memory_in[...].astype(F32)
        small_own[4 + MEM :, :] = jnp.zeros((small_own.shape[0] - 4 - MEM, part), F32)
        small_full[dp] = small_own[...]
        shard = [qkv_w[0], qkv_w[1], qkv_w[2], out_w[...].T]
        for g in range(4):
            ablk[g * part : (g + 1) * part, :] = shard[g][:, :128]
        for g in range(2):
            ablk[(4 + g) * part : (5 + g) * part, :] = jnp.concatenate(
                [shard[2 * g][:, 128:], shard[2 * g + 1][:, 128:]], axis=1
            )
    last_start = jnp.int32(0)
    for t in range(n):
        last_start = jnp.where((resets[t] > 0) & (t <= mp), t, last_start)
    cut = resets[mp] < 0
    for q in range(n):
        cut = cut | (mp - last_start == q * truncation[0])
    starts = jnp.full((PAD, hid.shape[1]), jnp.where(resets[mp] > 0, 1.0, 0.0)) > 0
    carries = jnp.full((PAD, hid.shape[1]), jnp.where((resets[mp] > 0) | cut, 0.0, 1.0)) > 0
    spare = lax.broadcasted_iota(jnp.int32, (1, PAD), 1)
    kbias[:, 0:SEG] = jnp.where(key_mask[pl.ds(mp, 1), :] > 0, 0.0, -1e30)
    kbias[:, SEG:] = jnp.where(spare < MEM, 0.0, -1e30)

    @pl.when(mp == 0)
    def _():
        mem_recv[...] = jnp.zeros_like(mem_recv)

    @pl.when(mp == n - 1)
    def _():
        for ref in (nlow, mixed, g2low, g1low, hat2):
            ref[mem_rows, :] = jnp.zeros((PAD, width), ref.dtype)
        for j in range(parts):
            act[j, mem_rows, :] = jnp.zeros((PAD, width), BF16)
            ginner[j, mem_rows, :] = jnp.zeros((PAD, width), BF16)
        dqkv[0, mem_rows, :] = jnp.zeros((PAD, width), BF16)

    barrier = pltpu.get_barrier_semaphore()
    friends = [(dp, lax.rem(mp + step, n)) for step in range(1, n)]
    if fused:
        friends += [(lax.rem(dp + step, m), mp) for step in range(1, m)]
    for friend in friends:
        pl.semaphore_signal(barrier, inc=1, device_id=friend, device_id_type=MESH)
    pl.semaphore_wait(barrier, len(friends))

    if fused:
        events, finish_gather = gather_events(at, (ablk, up_w, down_w), fulls, gsems)
        small_copies = []
        for step in range(1, m):
            copy = remote(small_full.at[dp], small_full.at[dp], small_send.at[step - 1],
                          small_recv.at[step - 1], (lax.rem(dp + step, m), mp))
            copy.start()
            small_copies.append(copy)
        for event in events[:7]:
            event()
        for copy in small_copies:
            copy.wait()
        small[...] = jnp.concatenate([small_full[i] for i in range(m)], axis=1)
        later = list(events[7:])

        @pl.loop(0, m)
        def _(i):
            rows = pl.ds(pl.multiple_of(i * part, part), part)
            a = [afull[j, i // 4, lax.rem(i // 2, 2), lax.rem(i, 2)] for j in range(n)]
            for g in range(4):
                pieces = []
                for j in range(n):
                    pieces.append(a[j][g * part : (g + 1) * part])
                    low = (4 + g // 2) * part
                    pieces.append(a[j][low : low + part, (g % 2) * HD : (g % 2 + 1) * HD])
                row = jnp.concatenate(pieces, axis=1)
                if g < 3:
                    wqkv[g, rows, :] = row
                else:
                    wot[rows, :] = row
    else:
        small[...] = small_in[...]
        loads = [
            pltpu.make_async_copy(src, dst, w_sem.at[i])
            for i, (src, dst) in enumerate(zip(weights_hbm, (wqkv, wot, wup, wdnt)))
        ]
        for load in loads:
            load.start()
        for load in loads:
            load.wait()
        later = []
    load_cot.start()

    def onward(count):
        for event in later[:count]:
            event()
        del later[:count]

    gain1, bias1 = small[0:1], small[1:2]
    gain2, bias2 = small[2:3], small[3:4]
    lane = lax.broadcasted_iota(jnp.int32, (1, 128), 1)
    half_scaled = [
        jnp.where(lane < HD, HD**-0.5, 0.0).astype(BF16),
        jnp.where(lane < HD, 0.0, HD**-0.5).astype(BF16),
    ]
    half_one = [
        jnp.where(lane < HD, 1.0, 0.0).astype(BF16),
        jnp.where(lane < HD, 0.0, 1.0).astype(BF16),
    ]
    head_of = lax.broadcasted_iota(jnp.int32, (1, width), 1) // HD

    def head_mask(h, value):
        return jnp.where(head_of == h, value, 0.0)

    def project(rows):
        x = hid[rows, :]
        for g in range(3):
            qkv[g, rows, :] = nn(x, wqkv[g]).astype(BF16)

    def softmax(scores):
        e = jnp.exp(scores - jnp.max(scores, axis=-1, keepdims=True))
        return (e * (1.0 / jnp.sum(e, axis=-1, keepdims=True))).astype(BF16)

    lane_full = lax.broadcasted_iota(jnp.int32, (SEG, 128), 1)
    first_half = lane_full < HD

    def attend_pair(pair):
        lanes = slice(pair * 128, (pair + 1) * 128)
        q = qkv[0, tok_rows, lanes]
        k = qkv[1, tok_rows, lanes]
        v = qkv[2, tok_rows, lanes]
        outs = []
        kept = stats[...]
        for half in range(2):
            h = 2 * pair + half
            scores = nt(q * half_scaled[half], k) + kbias[:, 0:SEG]
            top = jnp.max(scores, axis=-1, keepdims=True)
            e = jnp.exp(scores - top)
            kept = jnp.where(lane_full == h, top, kept)
            kept = jnp.where(lane_full == HD + h, jnp.sum(e, axis=-1, keepdims=True), kept)
            e = e.astype(BF16)
            probs[h] = e
            outs.append(nn(e, v))
        stats[...] = kept
        hat1[tok_rows, lanes] = jnp.where(first_half, outs[0], outs[1])

    def attend_to_memory():
        spread(kall, qkv[1, mem_rows, :], HD**-0.5)
        spread(vall, qkv[2, mem_rows, :], 1.0)
        kept = stats[...].T
        top_tokens, sum_tokens = kept[0:heads], kept[HD : HD + heads]
        scores = nt(kall[...], qkv[0, tok_rows, :]).reshape(heads, PAD, SEG)
        key = lax.broadcasted_iota(jnp.int32, (heads, PAD, SEG), 1)
        scores = jnp.where(key < MEM, scores, -1e30)
        top = jnp.maximum(top_tokens, jnp.max(scores, axis=1))
        e = jnp.exp(scores - top[:, None, :])
        scale = jnp.exp(top_tokens - top)
        inverse = 1.0 / (scale * sum_tokens + jnp.sum(e, axis=1))
        pmemory[...] = (e * inverse[:, None, :]).reshape(heads * PAD, SEG).astype(BF16)
        rest = jnp.zeros((128 - heads, SEG), F32)
        stats[...] = jnp.concatenate([scale * inverse, rest], axis=0).T
        extra = tn(pmemory[...], vall[...])
        for pair in range(pairs):
            lanes = slice(pair * 128, (pair + 1) * 128)
            mixed[tok_rows, lanes] = (
                hat1[tok_rows, lanes] * pair_scale(pair) + extra[:, lanes]
            ).astype(BF16)

    def pair_scale(pair):
        return jnp.where(
            first_half, stats[:, 2 * pair : 2 * pair + 1], stats[:, 2 * pair + 1 : 2 * pair + 2]
        )

    def spread(ref, x, value):
        for h in range(heads):
            ref[h * PAD : (h + 1) * PAD, :] = x * head_mask(h, value).astype(BF16)

    def gathered_heads(x):
        return sum(x[h * PAD : (h + 1) * PAD, :] * head_mask(h, 1.0) for h in range(heads))

    def attend_memory():
        spread(qall, qkv[0, mem_rows, :], HD**-0.5)
        p = softmax(nt(qall[...], qkv[1]) + kbias[...])
        pmem[...] = p
        mixed[mem_rows, :] = gathered_heads(nn(p, qkv[2])).astype(BF16)

    def each_part(rows, body):
        if rows is mem_rows:
            for j in range(parts):
                body(j)
        else:
            pl.loop(0, parts)(body)

    def feed(rows):
        resid = hid[rows, :].astype(F32) + nt(mixed[rows, :], wot[...])
        h1, i1 = normalize(resid)
        hat1[rows, :] = h1
        inv[rows, 0:1] = i1
        norm_one = h1 * gain1 + bias1
        nlow[rows, :] = norm_one.astype(BF16)
        hat2[rows, :] = norm_one

        def step(j):
            inner = nn(nlow[rows, :], wup[j])
            cumulative = 0.5 * (1.0 + lax.erf(inner * 0.7071067811865476))
            density = jnp.exp(-0.5 * inner * inner) * 0.3989422804014327
            a = (inner * cumulative).astype(BF16)
            act[j, rows, :] = a
            slope[j, rows, :] = (cumulative + inner * density).astype(BF16)
            hat2[rows, :] += nt(a, wdnt[j])

        each_part(rows, step)
        h2, i2 = normalize(hat2[rows, :])
        hat2[rows, :] = h2
        inv[rows, 1:2] = i2
        return (h2 * gain2 + bias2).astype(BF16)

    def feed_back(rows, grad_final):
        h2 = hat2[rows, :]
        dnorm[2:3, :] += jnp.sum(grad_final * h2, axis=0, keepdims=True)
        dnorm[3:4, :] += jnp.sum(grad_final, axis=0, keepdims=True)
        g2 = normalize_back(grad_final, h2, inv[rows, 1:2], gain2)
        g2low[rows, :] = g2.astype(BF16)
        gone[rows, :] = g2

        def step(j):
            gi = (nn(g2low[rows, :], wdnt[j]) * slope[j, rows, :].astype(F32)).astype(BF16)
            ginner[j, rows, :] = gi
            gone[rows, :] += nt(gi, wup[j])

        each_part(rows, step)
        grad_norm = gone[rows, :]
        h1 = hat1[rows, :]
        dnorm[0:1, :] += jnp.sum(grad_norm * h1, axis=0, keepdims=True)
        dnorm[1:2, :] += jnp.sum(grad_norm, axis=0, keepdims=True)
        g1 = normalize_back(grad_norm, h1, inv[rows, 0:1], gain1)
        gone[rows, :] = g1
        low = g1.astype(BF16)
        g1low[rows, :] = low
        gmix[rows, :] = nn(low, wot[...]).astype(BF16)

    def memory_keys_back():
        dprob = nt(vall[...], gmix[tok_rows, :]).reshape(heads, PAD, SEG)
        product = gmix[tok_rows, :].astype(F32) * mixed[tok_rows, :].astype(F32)
        high = product.astype(BF16)
        low = (product - high.astype(F32)).astype(BF16)
        row = lax.broadcasted_iota(jnp.int32, (16, width), 0)
        ones = jnp.where(head_of == row, 1.0, 0.0).astype(BF16)
        delta = (nt(ones, high) + nt(ones, low))[0:heads]
        probs_memory = pmemory[...].astype(F32).reshape(heads, PAD, SEG)
        ds = (probs_memory * (dprob - delta[:, None, :])).reshape(heads * PAD, SEG).astype(BF16)
        dk = gathered_heads(nn(ds, qkv[0, tok_rows, :])) * HD**-0.5
        dqkv[1, mem_rows, :] = dk.astype(BF16)
        dqkv[2, mem_rows, :] = gathered_heads(nn(pmemory[...], gmix[tok_rows, :])).astype(BF16)
        dqkv[0, tok_rows, :] = tn(ds, kall[...]).astype(BF16)

    def attend_back():
        for pair in range(pairs):
            lanes = slice(pair * 128, (pair + 1) * 128)
            scaled = gmix[tok_rows, lanes].astype(F32) * pair_scale(pair)
            gmix[tok_rows, lanes] = scaled.astype(BF16)

        @pl.loop(0, pairs)
        def _(pair):
            lanes = pl.ds(pl.multiple_of(pair * 128, 128), 128)
            q = qkv[0, tok_rows, lanes]
            k = qkv[1, tok_rows, lanes]
            v = qkv[2, tok_rows, lanes]
            g = gmix[tok_rows, lanes]
            product = g.astype(F32) * mixed[tok_rows, lanes].astype(F32)
            dqs = []
            dk = None
            dv = None
            for half in range(2):
                e = probs[2 * pair + half]
                gh = g * half_one[half]
                inside = first_half if half == 0 else ~first_half
                delta = jnp.sum(jnp.where(inside, product, 0.0), axis=-1, keepdims=True)
                ds = (e.astype(F32) * (nt(gh, v) - delta)).astype(BF16)
                dv_h = tn(e, gh)
                dk_h = tn(ds, q * half_scaled[half])
                dqs.append(nn(ds, k))
                dk = dk_h if dk is None else dk + dk_h
                dv = dv_h if dv is None else dv + dv_h
            dq = jnp.where(first_half, dqs[0], dqs[1]) * HD**-0.5
            dq += dqkv[0, tok_rows, lanes].astype(F32)
            dqkv[0, tok_rows, lanes] = dq.astype(BF16)
            dqkv[1, tok_rows, lanes] = dk.astype(BF16)
            dqkv[2, tok_rows, lanes] = dv.astype(BF16)

    def more(g, rows, extra):
        dqkv[g, rows, :] = (dqkv[g, rows, :].astype(F32) + extra).astype(BF16)

    def attend_back_memory():
        spread(qall, qkv[0, mem_rows, :], HD**-0.5)
        spread(gall, gmix[mem_rows, :], 1.0)
        dprob = nt(gall[...], qkv[2])
        pf = pmem[...].astype(F32)
        delta = jnp.sum(pf * dprob, axis=-1, keepdims=True)
        ds = (pf * (dprob - delta)).astype(BF16)
        dqkv[0, mem_rows, :] = (gathered_heads(nn(ds, qkv[1])) * HD**-0.5).astype(BF16)
        more(1, mem_rows, tn(ds[:, SEG:], qall[...]))
        more(2, mem_rows, tn(pmem[:, SEG:], gall[...]))
        probs[0, 0 : heads * PAD, :] = ds[:, 0:SEG]

    def attend_back_tokens():
        more(1, tok_rows, tn(probs[0, 0 : heads * PAD, :], qall[...]))
        more(2, tok_rows, tn(pmem[:, 0:SEG], gall[...]))

    def chain_copy(src, dst, slot, peer):
        return remote(src, dst, chain_sem.at[2 * slot], chain_sem.at[2 * slot + 1], (dp, peer))

    forward_copy = chain_copy(mem_send, mem_recv, 0, lax.rem(mp + 1, n))
    backward_copy = chain_copy(gm_send, gm_recv, 1, lax.rem(mp + n - 1, n))

    def take_memory():
        memory = small[4 : 4 + MEM, :]
        memory = jnp.concatenate([memory, jnp.zeros((PAD - MEM, width), F32)], axis=0)
        memory = jnp.where(starts, memory, mem_recv[...].astype(F32))
        hid[mem_rows, :] = memory.astype(BF16)
        project(mem_rows)

    load_tok.wait()
    onward(1)
    for c in range(2):
        project(pl.ds(c * 256, 256))
        onward(1)
    stats[...] = jnp.zeros_like(stats)
    for pair in range(pairs):
        attend_pair(pair)
        if pair == 3:

            @pl.when(mp == 0)
            def _():
                take_memory()
                attend_memory()

        if pair % 2 == 0:
            onward(1)
    onward(len(later))

    @pl.when(mp > 0)
    def _():
        forward_copy.wait_recv()
        take_memory()

    @pl.when((mp > 0) & (mp < n - 1))
    def _():
        attend_memory()

    @pl.when(mp < n - 1)
    def _():
        mem_send[...] = feed(mem_rows)
        forward_copy.start()

    attend_to_memory()

    @pl.loop(0, 2)
    def _(c):
        rows = pl.ds(pl.multiple_of(c * 256, 256), 256)
        lout[rows, :] = feed(rows)

    own = pl.ds(mp * SEG, SEG)
    keep_out = pltpu.make_async_copy(lout.at[tok_rows], lo_hbm.at[own], lo_sem)
    keep_out.start()
    keep_out.wait()
    out_copies = []
    size = SEG // PIECES

    def send_out(first, last):
        for piece in range(first, last):
            for step in (3, 2, 1):
                rows = pl.ds(mp * SEG + piece * size, size)
                copy = remote(lo_hbm.at[rows], lo_hbm.at[rows], lo_send.at[piece, step - 1],
                              lo_recv.at[piece, step - 1], (dp, at["z"][step]))
                copy.start()
                out_copies.append(copy)

    send_out(0, 3)

    dnorm[...] = jnp.zeros_like(dnorm)
    load_cot.wait()

    @pl.loop(0, 2)
    def _(c):
        rows = pl.ds(pl.multiple_of(c * 256, 256), 256)
        feed_back(rows, cot[rows, :].astype(F32))

    def input_grad(rows):
        return (
            gone[rows, :]
            + nt(dqkv[0, rows, :], wqkv[0])
            + nt(dqkv[1, rows, :], wqkv[1])
            + nt(dqkv[2, rows, :], wqkv[2])
        )

    def give_memory_grad():
        gmem = input_grad(mem_rows)
        gm_send[...] = jnp.where(carries, gmem, 0.0).astype(BF16)

        @pl.when(mp > 0)
        def _():
            backward_copy.start()

        dmem[...] = jnp.where(starts, gmem, 0.0)

    memory_keys_back()

    @pl.when(mp == n - 1)
    def _():
        give_memory_grad()

    attend_back()

    @pl.when(mp < n - 1)
    def _():
        backward_copy.wait_recv()
        feed_back(mem_rows, gm_recv[...].astype(F32))
        attend_back_memory()
        give_memory_grad()

    send_out(3, 4)
    cols = width // n
    for i in range(m):
        tiny[i, 0:MEM, :] = dmem[0:MEM, i * part : (i + 1) * part]
        tiny[i, MEM:, :] = dnorm[0:4, i * part : (i + 1) * part]
    dx_copies = []

    def tokens_back():
        @pl.when(mp < n - 1)
        def _():
            attend_back_tokens()

        for c in range(2):
            rows = pl.ds(c * 256, 256)
            g = gone[rows, :].T
            for j in range(3):
                g += nt(wqkv[j], dqkv[j, rows, :])
            g = g.astype(BF16)
            for j in range(n):
                dxs[j, :, rows] = g[j * cols : (j + 1) * cols]

        keep_dx = pltpu.make_async_copy(dxs.at[mp], dx_hbm.at[mp], dx_sem)
        keep_dx.start()
        dx_copies.append(keep_dx)
        for step in range(1, n):
            peer = at['z'][step]
            copy = remote(dxs.at[peer], dx_hbm.at[mp], dx_send.at[step - 1],
                          dx_recv.at[step - 1], (dp, peer))
            copy.start()
            dx_copies.append(copy)

    def in_thirds(body):
        @pl.loop(0, width // 256)
        def _(i):
            body(pl.ds(pl.multiple_of(i * 256, 256), 256))

    def down_grad(j):
        def third(some):
            wdnt[j, some, :] = tn(g2low[:, some], act[j]).astype(BF16)

        in_thirds(third)

    def up_grad(j):
        def third(some):
            wup[j, some, :] = tn(nlow[:, some], ginner[j]).astype(BF16)

        in_thirds(third)

    def attend_grads():
        def third(some):
            wot[some, :] = tn(g1low[:, some], mixed[...]).astype(BF16)
            for g in range(3):
                wqkv[g, some, :] = tn(hid[:, some], dqkv[g]).astype(BF16)

        in_thirds(third)

    if fused:
        finish_gather()
        tiny_start, tiny_end = tiny_steps(at, tiny, tsum, trecv, t_send, t_recv)
        f1, fetch, f2, f3, f4, total_of, finish_scatter = scatter_steps(
            at, (dfull, ufull, afull), firsts, rings, r2x, r2y, r3x, r3y, r4, ssems
        )
        tiny_start(0)
        order = (3, 2, 1, 0)
        for s in range(15):
            if s < 4:
                down_grad(at["z"][order[s]])
            elif s < 8:
                up_grad(at["z"][order[s - 4]])
            elif s == 8:
                tokens_back()
                attend_grads()

                @pl.loop(0, m)
                def _(i):
                    rows = pl.ds(pl.multiple_of(i * part, part), part)
                    w = [wqkv[g, rows, :] if g < 3 else wot[rows, :] for g in range(4)]
                    for j in range(n):
                        lo = j * cols
                        spot = afull.at[j, i // 4, lax.rem(i // 2, 2), lax.rem(i, 2)]
                        for g in range(4):
                            spot[g * part : (g + 1) * part, :] = w[g][:, lo : lo + 128]
                        for g in range(2):
                            spot[(4 + g) * part : (5 + g) * part, :] = jnp.concatenate(
                                [w[2 * g][:, lo + 128 : lo + cols],
                                 w[2 * g + 1][:, lo + 128 : lo + cols]],
                                axis=1,
                            )

            if s in (0, 2, 4, 6):
                send_out(s // 2 + 4, s // 2 + 5)
            if s < 12:
                f1(s)
            if 1 <= s < 13:
                fetch(s - 1)
            if 2 <= s < 14:
                f3(s - 2)
            if 3 <= s:
                f4(s - 3)
            if 1 <= s < 13:
                f2(s - 1)
            if s < 5:
                tiny_end(s)
                if s < 4:
                    tiny_start(s + 1)
        done = tsum[0, dp]
        dmem_out[...] = done[0:MEM]
        for i in range(4):
            dnorm_out[i][...] = done[MEM + i : MEM + i + 1]
        ddown_out[...] = total_of(0)
        dup_out[...] = total_of(1)
        a = total_of(2)
        for g in range(4):
            edge = a[(4 + g // 2) * part : (5 + g // 2) * part, (g % 2) * HD : (g % 2 + 1) * HD]
            block = jnp.concatenate([a[g * part : (g + 1) * part], edge], axis=1)
            if g < 3:
                dqkv_out[g] = block
            else:
                dout_out[...] = block.T
        finish_scatter()
    else:
        send_out(4, PIECES)
        tokens_back()
        pl.loop(0, parts)(down_grad)
        pl.loop(0, parts)(up_grad)
        attend_grads()
        stores = [
            pltpu.make_async_copy(src, dst, w_sem.at[i])
            for i, (src, dst) in enumerate(zip((wqkv, wot, wup, wdnt), grads_hbm))
        ]
        for store in stores:
            store.start()
        for store in stores:
            store.wait()
    for copy in out_copies + dx_copies:
        copy.wait()

    @pl.when(mp < n - 1)
    def _():
        forward_copy.wait_send()

    @pl.when(mp > 0)
    def _():
        backward_copy.wait_send()


def run_layer(n, m, fused, tokens, cotangent, resets, truncation, key_mask, *rest):
    width = tokens.shape[1]
    parts = n
    heads = width // HD
    part = width // m
    vmem = pl.BlockSpec(memory_space=pltpu.VMEM)
    smem = pl.BlockSpec(memory_space=pltpu.SMEM)
    anyspace = pl.BlockSpec(memory_space=pl.ANY)
    sems = pltpu.SemaphoreType.DMA
    out_shape = [
        jax.ShapeDtypeStruct((n * SEG, width), BF16),
        jax.ShapeDtypeStruct((n, width // n, SEG), BF16),
    ]
    if fused:
        pieces = [(6 * part, 128), (part, width), (part, width)]
        backward = [pieces[2], pieces[1], pieces[0]]
        out_shape += [jax.ShapeDtypeStruct((4, 2, 2) + p, BF16) for p in backward]
        out_shape += [jax.ShapeDtypeStruct(w.shape, F32) for w in rest[5:]]
        out_shape += [jax.ShapeDtypeStruct((MEM, part), F32)]
        out_shape += [jax.ShapeDtypeStruct((1, part), F32)] * 4
        in_rest = [vmem] * len(rest)
        out_specs = [anyspace] * 5 + [vmem] * 9
        first = (
            [pltpu.VMEM((m, 32, part), F32), pltpu.VMEM((32, part), F32),
             pltpu.VMEM(pieces[0], BF16)]
            + [pltpu.VMEM((4, 2, 2, 2) + p, BF16) for p in pieces]
            + gather_sems(3)
            + [sems((m - 1,)), sems((m - 1,))]
            + [pltpu.VMEM((3, width, width), BF16), pltpu.VMEM((width, width), BF16)]
            + [pltpu.VMEM((2, 2) + pieces[0], BF16)]
            + scatter_scratch(backward)
            + [pltpu.VMEM((m, MEM + 4, part), F32), pltpu.VMEM((2, m, MEM + 4, part), F32),
               pltpu.VMEM((5, m, MEM + 4, part), F32), sems((5,)), sems((5,))]
        )
    else:
        shapes = [w.shape for w in rest[1:]]
        out_shape += [jax.ShapeDtypeStruct(s, BF16) for s in shapes]
        out_shape += [jax.ShapeDtypeStruct((m, MEM + 4, part), F32)]
        in_rest = [vmem] + [anyspace] * 4
        out_specs = [anyspace] * 6 + [vmem]
        first = [pltpu.VMEM(s, BF16) for s in shapes]
    row_bf = pltpu.VMEM((ROWS, width), BF16)
    row_f = pltpu.VMEM((ROWS, width), F32)
    one_f = pltpu.VMEM((ROWS, 2), F32)
    wide = pltpu.VMEM((parts, ROWS, width), BF16)
    mem_bf = pltpu.VMEM((PAD, width), BF16)
    all_bf = pltpu.VMEM((heads * PAD, width), BF16)
    return pl.pallas_call(
        functools.partial(layer_kernel, n, m, fused),
        out_shape=tuple(out_shape),
        in_specs=[anyspace, anyspace, smem, smem, vmem] + in_rest,
        out_specs=tuple(out_specs),
        scratch_shapes=first + [
            pltpu.VMEM((1, ROWS), F32), pltpu.VMEM((32, width), F32),
            pltpu.VMEM((heads * PAD, ROWS), BF16), all_bf, all_bf,
            pltpu.VMEM((heads * PAD, SEG), BF16), pltpu.VMEM((SEG, 128), F32),
            row_bf, pltpu.VMEM((SEG, width), BF16), pltpu.VMEM((3, ROWS, width), BF16),
            pltpu.VMEM((heads, SEG, SEG), BF16), row_bf, row_f, one_f, row_bf, wide, wide, row_f,
            row_bf, row_bf, row_bf, pltpu.VMEM((3, ROWS, width), BF16),
            pltpu.VMEM((n, width // n, SEG), BF16),
            pltpu.VMEM((8, width), F32), pltpu.VMEM((PAD, width), F32),
            mem_bf, mem_bf, mem_bf, mem_bf,
            sems((2,)), sems((4,)), sems, sems, sems((PIECES, n - 1)), sems((PIECES, n - 1)), sems((n - 1,)),
            sems((n - 1,)), sems((4,)),
        ],
        compiler_params=pltpu.CompilerParams(
            collective_id=0, has_side_effects=True, vmem_limit_bytes=255 * 2**18
        ),
        cost_estimate=pl.CostEstimate(
            flops=26_000_000_000, bytes_accessed=40_000_000, transcendentals=10_000_000
        ),
    )(tokens, cotangent, resets, truncation, key_mask, *rest)


def finish_kernel(lo_in, dx_in, *refs):
    count = (len(refs) - 5) // 2
    lo_out, dx_out, held, sem_in, sem_out = refs[count], refs[count + 1], *refs[-3:]
    pieces, size = held.shape[:2]
    loads = [
        pltpu.make_async_copy(lo_in.at[pl.ds(i * size, size)], held.at[i], sem_in.at[i])
        for i in range(pieces)
    ]
    stores = [
        pltpu.make_async_copy(held.at[i], lo_out.at[pl.ds(i * size, size)], sem_out.at[i])
        for i in range(pieces)
    ]
    for load in loads:
        load.start()
    for j in range(dx_in.shape[0]):
        dx_out[:, j * SEG : (j + 1) * SEG] = dx_in[j].astype(F32)
    for src, dst in zip(refs[:count], refs[count + 2 : -3]):
        dst[...] = src[...]
    for load, store in zip(loads, stores):
        load.wait()
        store.start()
    for store in stores:
        store.wait()


def finish_outputs(lo, dx, *rest):
    vmem = pl.BlockSpec(memory_space=pltpu.VMEM)
    anyspace = pl.BlockSpec(memory_space=pl.ANY)
    n, cols, rows = dx.shape
    return pl.pallas_call(
        finish_kernel,
        out_shape=(
            jax.ShapeDtypeStruct(lo.shape, lo.dtype),
            jax.ShapeDtypeStruct((cols, n * rows), F32),
            *[jax.ShapeDtypeStruct(r.shape, r.dtype) for r in rest],
        ),
        in_specs=[anyspace] + [vmem] * (1 + len(rest)),
        out_specs=(anyspace,) + (vmem,) * (1 + len(rest)),
        scratch_shapes=[
            pltpu.VMEM((n, lo.shape[0] // n, lo.shape[1]), BF16),
            pltpu.SemaphoreType.DMA((n,)),
            pltpu.SemaphoreType.DMA((n,)),
        ],
        compiler_params=pltpu.CompilerParams(vmem_limit_bytes=60 * 2**20),
    )(lo, dx, *rest)


def shards(
    tokens, cotangent, resets, key_mask, truncation_segments, qkv_weight, out_weight, up_weight,
    down_weight, memory_init, norm1_gain, first_norm_bias, norm2_gain, norm2_bias,
):
    n = lax.axis_size("mp")
    m = lax.axis_size("dp")
    width = tokens.shape[1]
    slots = resets.shape[0]
    rows = width // m
    cols = width // n
    if m == 8 and n == 4 and width == 768:
        out = run_layer(
            n, m, True, tokens, cotangent, resets, truncation_segments,
            key_mask.reshape(slots, SEG), norm1_gain[None], first_norm_bias[None],
            norm2_gain[None], norm2_bias[None], memory_init, qkv_weight, out_weight, up_weight,
            down_weight.T,
        )
        lo, dx, *rest = finish_outputs(*out[:2], *out[5:])
        return (lo, dx.T, *rest[:3], rest[3].T, rest[4], *[d[0] for d in rest[5:]])
    small = jnp.concatenate(
        [norm1_gain[None], first_norm_bias[None], norm2_gain[None], norm2_bias[None], memory_init,
         jnp.zeros((32 - 4 - MEM, rows), BF16)],
        axis=0,
    )
    block = jnp.concatenate([qkv_weight, out_weight.T[None]], axis=0)
    block = lax.all_gather(block, ("mp", "dp"), axis=0)
    block = block.reshape(n, m, 4, rows, cols).transpose(2, 1, 3, 0, 4).reshape(4, width, width)
    wup = lax.all_gather(up_weight, ("mp", "dp"), axis=0).reshape(n, width, -1)
    wdnt = lax.all_gather(down_weight.T, ("mp", "dp"), axis=0).reshape(n, width, -1)
    small = lax.all_gather(small, "dp", axis=1, tiled=True).astype(F32)
    lo, dx, dqkv, dot_w, dup, ddnt, tiny = run_layer(
        n, m, False, tokens, cotangent, resets, truncation_segments, key_mask.reshape(slots, SEG),
        small, block[:3], block[3], wup, wdnt,
    )
    dblock = jnp.concatenate([dqkv, dot_w[None]], axis=0)
    dblock = dblock.reshape(4, m, rows, n, cols).transpose(3, 1, 0, 2, 4)
    dblock = dblock.reshape(n * m, 4, rows, cols)
    dblock = lax.psum_scatter(dblock, ("mp", "dp"), scatter_dimension=0).astype(F32)
    dup = lax.psum_scatter(
        dup.reshape(n * m, rows, -1), ("mp", "dp"), scatter_dimension=0
    ).astype(F32)
    ddnt = lax.psum_scatter(
        ddnt.reshape(n * m, rows, -1), ("mp", "dp"), scatter_dimension=0
    ).astype(F32)
    tiny = lax.psum(tiny, ("mp", "dp"))[lax.axis_index("dp")]
    return (
        lo,
        dx.astype(F32).transpose(0, 2, 1).reshape(n * SEG, cols),
        dblock[:3],
        dblock[3].T,
        dup,
        ddnt.T,
        tiny[:MEM],
        tiny[MEM],
        tiny[MEM + 1],
        tiny[MEM + 2],
        tiny[MEM + 3],
    )


def solution(mesh):
    return jax.shard_map(
        shards,
        mesh=mesh,
        in_specs=(
            P("dp", None), P("dp", None), P("dp"), P("dp"), P(),
            P(None, "dp", "mp"), P("mp", "dp"), P("dp", "mp"), P("mp", "dp"), P(None, "dp"),
            P("dp"), P("dp"), P("dp"), P("dp"),
        ),
        out_specs=(
            P("dp", None), P("dp", "mp"), P(None, "dp", "mp"), P("mp", "dp"), P("dp", "mp"),
            P("mp", "dp"), P(None, "dp"), P("dp"), P("dp"), P("dp"), P("dp"),
        ),
        check_vma=False,
    )
```

```python
import functools

import jax
import jax.numpy as jnp
from jax import lax
from jax.experimental import pallas as pl
from jax.experimental.pallas import tpu as pltpu
from jax.sharding import PartitionSpec as P

HD = 64
SEG = 512
MEM = 20
PAD = 32
ROWS = SEG + PAD
PIECES = 16
EPSILON = 1e-05
MESH = pl.DeviceIdType.MESH
F32 = jnp.float32
BF16 = jnp.bfloat16


def nn(a, b):
    return lax.dot_general(a, b, (((1,), (0,)), ((), ())), preferred_element_type=F32)


def nt(a, b):
    return lax.dot_general(a, b, (((1,), (1,)), ((), ())), preferred_element_type=F32)


def tn(a, b):
    return lax.dot_general(a, b, (((0,), (0,)), ((), ())), preferred_element_type=F32)


def normalize(resid):
    center = resid - jnp.mean(resid, axis=-1, keepdims=True)
    inverse = lax.rsqrt(jnp.mean(center * center, axis=-1, keepdims=True) + EPSILON)
    return center * inverse, inverse


def normalize_back(grad_out, hat, inverse, gain):
    grad_hat = grad_out * gain
    return inverse * (
        grad_hat
        - jnp.mean(grad_hat, axis=-1, keepdims=True)
        - hat * jnp.mean(grad_hat * hat, axis=-1, keepdims=True)
    )


def place(n):
    dp = lax.axis_index("dp")
    mp = lax.axis_index("mp")
    c, x, y = lax.rem(dp, 2), lax.rem(dp // 2, 2), dp // 4
    return {
        "c": c,
        "x": x,
        "y": y,
        "mp": mp,
        "core": (dp + 1 - 2 * c, mp),
        "xp": (dp + 2 - 4 * x, mp),
        "yp": (dp + 4 - 8 * y, mp),
        "z": [mp, mp + 1 - 2 * lax.rem(mp, 2), lax.rem(mp + 2, 4), 3 - mp],
        "dp": dp,
    }


def remote(src, dst, send, recv, peer):
    return pltpu.make_async_remote_copy(
        src_ref=src, dst_ref=dst, send_sem=send, recv_sem=recv, device_id=peer, device_id_type=MESH
    )


def gather_events(at, shards_in, fulls, sems):
    z_send, z_recv, s1_send, s1_recv, s2_send, s2_recv, c_send, c_recv, own_sem = sems
    c, x, y, mp = at["c"], at["x"], at["y"], at["mp"]
    mine, by_x, by_y, diag = (y, x), (y, 1 - x), (1 - y, x), (1 - y, 1 - x)
    kinds = len(shards_in)
    sent = []
    own = []

    def go(copy):
        copy.start()
        sent.append(copy)
        return copy

    def arrived(ref, sem):
        remote(ref, ref, s1_send.at[0, 0], sem, at["core"]).wait_recv()

    def start_z(t):
        for k in range(1, 4):
            go(remote(shards_in[t], fulls[t].at[mp, *mine, c], z_send.at[t, k - 1],
                      z_recv.at[t, k - 1], (at["dp"], at["z"][k])))

    def e1(t, k):
        s = 4 * t + k
        j = at["z"][k]
        full = fulls[t]
        piece = full.at[j, *mine, c]
        if k == 0:
            keep = pltpu.make_async_copy(shards_in[t], piece, own_sem.at[t])
            keep.start()
            own.append(keep)
            src = shards_in[t]
        else:
            arrived(piece, z_recv.at[t, k - 1])
            src = piece
        go(remote(src, piece, s1_send.at[s, 0], s1_recv.at[s, 0], at["xp"]))
        go(remote(src, piece, s1_send.at[s, 1], s1_recv.at[s, 1], at["yp"]))
        go(remote(src, piece, c_send.at[s, 0], c_recv.at[s, 0], at["core"]))

    def e2(t, k):
        s = 4 * t + k
        full = fulls[t]
        j = at["z"][k]
        half = full.shape[4] // 2
        px, py = full.at[j, *by_x, c], full.at[j, *by_y, c]
        arrived(px, s1_recv.at[s, 0])
        low = full.at[j, *by_x, c, pl.ds(0, half)]
        go(remote(low, low, s2_send.at[s, 1], s2_recv.at[s, 1], at["yp"]))
        go(remote(px, px, c_send.at[s, 1], c_recv.at[s, 1], at["core"]))
        arrived(py, s1_recv.at[s, 1])
        high = full.at[j, *by_y, c, pl.ds(half, half)]
        go(remote(high, high, s2_send.at[s, 0], s2_recv.at[s, 0], at["xp"]))
        go(remote(py, py, c_send.at[s, 2], c_recv.at[s, 2], at["core"]))

    def e3(t, k):
        s = 4 * t + k
        full = fulls[t]
        j = at["z"][k]
        half = full.shape[4] // 2
        arrived(full.at[j, *diag, c, pl.ds(half, half)], s2_recv.at[s, 0])
        arrived(full.at[j, *diag, c, pl.ds(0, half)], s2_recv.at[s, 1])
        pd = full.at[j, *diag, c]
        go(remote(pd, pd, c_send.at[s, 3], c_recv.at[s, 3], at["core"]))

    def e4(t, k):
        s = 4 * t + k
        full = fulls[t]
        j = at["z"][k]
        for q, spot in enumerate((mine, by_x, by_y, diag)):
            arrived(full.at[j, *spot, 1 - c], c_recv.at[s, q])
        if k == 0:
            own[t].wait()

    events = []
    order = [(t, k) for t in range(kinds) for k in range(4)]
    total = len(order)
    for s in range(total + 3):
        def event(s=s):
            if s == 0:
                start_z(0)
            if s % 4 == 1 and s // 4 + 1 < kinds:
                start_z(s // 4 + 1)
            if s < total:
                e1(*order[s])
            if 0 <= s - 1 < total:
                e2(*order[s - 1])
            if 0 <= s - 2 < total:
                e3(*order[s - 2])
            if 0 <= s - 3 < total:
                e4(*order[s - 3])
        events.append(event)

    def finish():
        for copy in sent:
            copy.wait_send()

    return events, finish


def gather_sems(kinds):
    sems = pltpu.SemaphoreType.DMA
    total = 4 * kinds
    return [
        sems((kinds, 3)), sems((kinds, 3)), sems((total, 2)), sems((total, 2)), sems((total, 2)),
        sems((total, 2)), sems((total, 4)), sems((total, 4)), sems((kinds,)),
    ]


def scatter_steps(at, fulls, firsts, rings, r2x, r2y, r3x, r3y, r4, sems):
    c_send, c_recv, l_sem, s1_send, s1_recv, s2_send, s2_recv, z_send, z_recv = sems
    c, x, y = at["c"], at["x"], at["y"]
    order = (3, 2, 1, 0)
    sent = []

    def go(copy):
        copy.start()
        sent.append(copy)

    def arrived(ref, sem):
        remote(ref, ref, c_send.at[0], sem, at["core"]).wait_recv()

    def spot(s):
        t, q = s // 4, s % 4
        return t, q, at["z"][order[q]], fulls[t].shape[4] // 2

    def load(s):
        t, q, _, _ = spot(s)
        return pltpu.make_async_copy(firsts[t].at[q], rings[t], l_sem.at[s])

    def f1(s):
        t, q, j, _ = spot(s)
        go(remote(fulls[t].at[j, :, :, 1 - c], firsts[t].at[q], c_send.at[s], c_recv.at[s],
                  at["core"]))

    def fetch(s):
        t, q, _, _ = spot(s)
        arrived(firsts[t].at[q], c_recv.at[s])
        load(s).start()

    def add(p, q):
        return (p.astype(F32) + q.astype(F32)).astype(BF16)

    def f2(s):
        t, q, j, half = spot(s)
        full = fulls[t]
        load(s).wait()
        for yy in range(2):
            for xx in range(2):
                full[j, yy, xx, c] = add(full[j, yy, xx, c], rings[t][yy, xx])
        go(remote(full.at[j, :, 1 - x, c, pl.ds(0, half)], r2x[t].at[q],
                  s1_send.at[s, 0], s1_recv.at[s, 0], at["xp"]))
        go(remote(full.at[j, 1 - y, :, c, pl.ds(half, half)], r2y[t].at[q],
                  s1_send.at[s, 1], s1_recv.at[s, 1], at["yp"]))

    def f3(s):
        t, q, j, half = spot(s)
        full = fulls[t]
        low, high = slice(0, half), slice(half, 2 * half)
        arrived(r2x[t].at[q], s1_recv.at[s, 0])
        for v in range(2):
            full[j, v, x, c, low] = add(full[j, v, x, c, low], r2x[t][q, v])
        go(remote(full.at[j, 1 - y, x, c, pl.ds(0, half)], r3y[t].at[q],
                  s2_send.at[s, 1], s2_recv.at[s, 1], at["yp"]))
        arrived(r2y[t].at[q], s1_recv.at[s, 1])
        for v in range(2):
            full[j, y, v, c, high] = add(full[j, y, v, c, high], r2y[t][q, v])
        go(remote(full.at[j, y, 1 - x, c, pl.ds(half, half)], r3x[t].at[q],
                  s2_send.at[s, 0], s2_recv.at[s, 0], at["xp"]))

    def f4(s):
        t, q, j, half = spot(s)
        full = fulls[t]
        k = order[q]
        low, high = slice(0, half), slice(half, 2 * half)
        arrived(r3y[t].at[q], s2_recv.at[s, 1])
        arrived(r3x[t].at[q], s2_recv.at[s, 0])
        full[j, y, x, c, low] = add(full[j, y, x, c, low], r3y[t][q])
        full[j, y, x, c, high] = add(full[j, y, x, c, high], r3x[t][q])
        if k:
            go(remote(full.at[j, y, x, c], r4[t].at[k - 1], z_send.at[t, k - 1],
                      z_recv.at[t, k - 1], (at["dp"], at["z"][k])))

    def total_of(t):
        got = fulls[t][at["mp"], y, x, c].astype(F32)
        for k in range(1, 4):
            arrived(r4[t].at[k - 1], z_recv.at[t, k - 1])
            got += r4[t][k - 1].astype(F32)
        return got

    def finish():
        for copy in sent:
            copy.wait_send()

    return f1, fetch, f2, f3, f4, total_of, finish


def scatter_scratch(shapes):
    sems = pltpu.SemaphoreType.DMA
    kinds = len(shapes)
    total = 4 * kinds

    def per(f):
        return [pltpu.VMEM(f(r, w), BF16) for r, w in shapes]

    return (
        per(lambda r, w: (4, 2, r // 2, w))
        + per(lambda r, w: (4, 2, r // 2, w))
        + per(lambda r, w: (4, r // 2, w))
        + per(lambda r, w: (4, r // 2, w))
        + per(lambda r, w: (3, r, w))
        + [sems((total,)), sems((total,)), sems((total,)), sems((total, 2)), sems((total, 2)),
           sems((total, 2)), sems((total, 2)), sems((kinds, 3)), sems((kinds, 3))]
    )


def tiny_steps(at, tiny, tsum, trecv, t_send, t_recv):
    peers = [at["core"], at["xp"], at["yp"], (at["dp"], at["z"][1]), (at["dp"], at["z"][2])]

    def copy(q):
        src = tiny if q == 0 else tsum.at[(q - 1) % 2]
        return remote(src, trecv.at[q], t_send.at[q], t_recv.at[q], peers[q])

    def end(q):
        copy(q).wait()
        tsum[q % 2] = (tiny[...] if q == 0 else tsum[(q - 1) % 2]) + trecv[q]

    return (lambda q: copy(q).start()), end


def layer_kernel(n, m, fused, *refs):
    at = place(n)
    dp, mp = lax.axis_index("dp"), lax.axis_index("mp")
    take = iter(refs)

    def some(count):
        return [next(take) for _ in range(count)]

    tok_hbm, cot_hbm, resets, truncation, key_mask = some(5)
    if fused:
        norm_in, (memory_in, qkv_w, out_w, up_w, down_w) = some(4), some(5)
        lo_hbm, dx_hbm = some(2)
        firsts = some(3)
        dqkv_out, dout_out, dup_out, ddown_out, dmem_out, *dnorm_out = some(9)
        small_full, small_own, ablk = some(3)
        fulls = some(3)
        gsems = some(9)
        small_send, small_recv = some(2)
        wqkv, wot, ring_a = some(3)
        r2x, r2y, r3x, r3y, r4 = [some(3) for _ in range(5)]
        ssems = some(9)
        tiny, tsum, trecv, t_send, t_recv = some(5)
        afull, ufull, dfull = fulls
        parts = n
        width = wot.shape[0]
        wup = ufull.reshape(n, width, width)
        wdnt = dfull.reshape(n, width, width)
    else:
        small_in, weights_hbm = next(take), some(4)
        lo_hbm, dx_hbm = some(2)
        grads_hbm, tiny = some(4), next(take)
        wqkv, wot, wup, wdnt = some(4)
    (
        kbias, small, pmem, kall, vall, pmemory, stats,
        hid, cot, qkv, probs, mixed, hat1, inv, nlow, act, slope, hat2,
        g2low, g1low, gmix, dqkv, dxs, dnorm, dmem,
        mem_recv, mem_send, gm_recv, gm_send,
        load_sem, w_sem, lo_sem, dx_sem, lo_send, lo_recv, dx_send, dx_recv, chain_sem,
    ) = some(38)
    qall, gall = kall, vall
    ginner, gone, lout = slope, hat2, gmix
    if fused:
        ring_b = cot.at[pl.ds(0, 4 * up_w.shape[0])].reshape(2, 2, *up_w.shape)
        rings = (ring_b, ring_b, ring_a)
    width = hid.shape[1]
    heads = width // HD
    pairs = width // 128
    parts = n
    part = width // m
    tok_rows = pl.ds(0, SEG)
    mem_rows = pl.ds(SEG, PAD)

    load_tok = pltpu.make_async_copy(
        tok_hbm.at[pl.ds(mp * SEG, SEG)], hid.at[tok_rows], load_sem.at[0]
    )
    load_cot = pltpu.make_async_copy(cot_hbm.at[pl.ds(mp * SEG, SEG)], cot, load_sem.at[1])
    load_tok.start()
    if fused:
        for i, ref in enumerate(norm_in):
            small_own[i : i + 1, :] = ref[...].astype(F32)
        small_own[4 : 4 + MEM, :] = memory_in[...].astype(F32)
        small_own[4 + MEM :, :] = jnp.zeros((small_own.shape[0] - 4 - MEM, part), F32)
        small_full[dp] = small_own[...]
        shard = [qkv_w[0], qkv_w[1], qkv_w[2], out_w[...].T]
        for g in range(4):
            ablk[g * part : (g + 1) * part, :] = shard[g][:, :128]
        for g in range(2):
            ablk[(4 + g) * part : (5 + g) * part, :] = jnp.concatenate(
                [shard[2 * g][:, 128:], shard[2 * g + 1][:, 128:]], axis=1
            )
    last_start = jnp.int32(0)
    for t in range(n):
        last_start = jnp.where((resets[t] > 0) & (t <= mp), t, last_start)
    cut = resets[mp] < 0
    for q in range(n):
        cut = cut | (mp - last_start == q * truncation[0])
    starts = jnp.full((PAD, hid.shape[1]), jnp.where(resets[mp] > 0, 1.0, 0.0)) > 0
    carries = jnp.full((PAD, hid.shape[1]), jnp.where((resets[mp] > 0) | cut, 0.0, 1.0)) > 0
    spare = lax.broadcasted_iota(jnp.int32, (1, PAD), 1)
    kbias[:, 0:SEG] = jnp.where(key_mask[pl.ds(mp, 1), :] > 0, 0.0, -1e30)
    kbias[:, SEG:] = jnp.where(spare < MEM, 0.0, -1e30)

    @pl.when(mp == 0)
    def _():
        mem_recv[...] = jnp.zeros_like(mem_recv)

    @pl.when(mp == n - 1)
    def _():
        for ref in (nlow, mixed, g2low, g1low, hat2):
            ref[mem_rows, :] = jnp.zeros((PAD, width), ref.dtype)
        for j in range(parts):
            act[j, mem_rows, :] = jnp.zeros((PAD, width), BF16)
            ginner[j, mem_rows, :] = jnp.zeros((PAD, width), BF16)
        dqkv[0, mem_rows, :] = jnp.zeros((PAD, width), BF16)

    barrier = pltpu.get_barrier_semaphore()
    friends = [(dp, lax.rem(mp + step, n)) for step in range(1, n)]
    if fused:
        friends += [(lax.rem(dp + step, m), mp) for step in range(1, m)]
    for friend in friends:
        pl.semaphore_signal(barrier, inc=1, device_id=friend, device_id_type=MESH)
    pl.semaphore_wait(barrier, len(friends))

    if fused:
        events, finish_gather = gather_events(at, (ablk, up_w, down_w), fulls, gsems)
        small_copies = []
        for step in range(1, m):
            copy = remote(small_full.at[dp], small_full.at[dp], small_send.at[step - 1],
                          small_recv.at[step - 1], (lax.rem(dp + step, m), mp))
            copy.start()
            small_copies.append(copy)
        for event in events[:7]:
            event()
        for copy in small_copies:
            copy.wait()
        small[...] = jnp.concatenate([small_full[i] for i in range(m)], axis=1)
        later = list(events[7:])

        @pl.loop(0, m)
        def _(i):
            rows = pl.ds(pl.multiple_of(i * part, part), part)
            a = [afull[j, i // 4, lax.rem(i // 2, 2), lax.rem(i, 2)] for j in range(n)]
            for g in range(4):
                pieces = []
                for j in range(n):
                    pieces.append(a[j][g * part : (g + 1) * part])
                    low = (4 + g // 2) * part
                    pieces.append(a[j][low : low + part, (g % 2) * HD : (g % 2 + 1) * HD])
                row = jnp.concatenate(pieces, axis=1)
                if g < 3:
                    wqkv[g, rows, :] = row
                else:
                    wot[rows, :] = row
    else:
        small[...] = small_in[...]
        loads = [
            pltpu.make_async_copy(src, dst, w_sem.at[i])
            for i, (src, dst) in enumerate(zip(weights_hbm, (wqkv, wot, wup, wdnt)))
        ]
        for load in loads:
            load.start()
        for load in loads:
            load.wait()
        later = []
    load_cot.start()

    def onward(count):
        for event in later[:count]:
            event()
        del later[:count]

    gain1, bias1 = small[0:1], small[1:2]
    gain2, bias2 = small[2:3], small[3:4]
    lane = lax.broadcasted_iota(jnp.int32, (1, 128), 1)
    half_scaled = [
        jnp.where(lane < HD, HD**-0.5, 0.0).astype(BF16),
        jnp.where(lane < HD, 0.0, HD**-0.5).astype(BF16),
    ]
    half_one = [
        jnp.where(lane < HD, 1.0, 0.0).astype(BF16),
        jnp.where(lane < HD, 0.0, 1.0).astype(BF16),
    ]
    head_of = lax.broadcasted_iota(jnp.int32, (1, width), 1) // HD

    def head_mask(h, value):
        return jnp.where(head_of == h, value, 0.0)

    def project(rows):
        x = hid[rows, :]
        for g in range(3):
            qkv[g, rows, :] = nn(x, wqkv[g]).astype(BF16)

    def softmax(scores):
        e = jnp.exp(scores - jnp.max(scores, axis=-1, keepdims=True))
        return (e * (1.0 / jnp.sum(e, axis=-1, keepdims=True))).astype(BF16)

    lane_full = lax.broadcasted_iota(jnp.int32, (SEG, 128), 1)
    first_half = lane_full < HD

    def attend_pair(pair):
        lanes = slice(pair * 128, (pair + 1) * 128)
        q = qkv[0, tok_rows, lanes]
        k = qkv[1, tok_rows, lanes]
        v = qkv[2, tok_rows, lanes]
        outs = []
        kept = stats[...]
        for half in range(2):
            h = 2 * pair + half
            scores = nt(q * half_scaled[half], k) + kbias[:, 0:SEG]
            top = jnp.max(scores, axis=-1, keepdims=True)
            e = jnp.exp(scores - top)
            kept = jnp.where(lane_full == h, top, kept)
            kept = jnp.where(lane_full == HD + h, jnp.sum(e, axis=-1, keepdims=True), kept)
            e = e.astype(BF16)
            probs[h] = e
            outs.append(nn(e, v))
        stats[...] = kept
        hat1[tok_rows, lanes] = jnp.where(first_half, outs[0], outs[1])

    def attend_to_memory():
        spread(kall, qkv[1, mem_rows, :], HD**-0.5)
        spread(vall, qkv[2, mem_rows, :], 1.0)
        kept = stats[...].T
        top_tokens, sum_tokens = kept[0:heads], kept[HD : HD + heads]
        scores = nt(kall[...], qkv[0, tok_rows, :]).reshape(heads, PAD, SEG)
        key = lax.broadcasted_iota(jnp.int32, (heads, PAD, SEG), 1)
        scores = jnp.where(key < MEM, scores, -1e30)
        top = jnp.maximum(top_tokens, jnp.max(scores, axis=1))
        e = jnp.exp(scores - top[:, None, :])
        scale = jnp.exp(top_tokens - top)
        inverse = 1.0 / (scale * sum_tokens + jnp.sum(e, axis=1))
        pmemory[...] = (e * inverse[:, None, :]).reshape(heads * PAD, SEG).astype(BF16)
        rest = jnp.zeros((128 - heads, SEG), F32)
        stats[...] = jnp.concatenate([scale * inverse, rest], axis=0).T
        extra = tn(pmemory[...], vall[...])
        for pair in range(pairs):
            lanes = slice(pair * 128, (pair + 1) * 128)
            mixed[tok_rows, lanes] = (
                hat1[tok_rows, lanes] * pair_scale(pair) + extra[:, lanes]
            ).astype(BF16)

    def pair_scale(pair):
        return jnp.where(
            first_half, stats[:, 2 * pair : 2 * pair + 1], stats[:, 2 * pair + 1 : 2 * pair + 2]
        )

    def spread(ref, x, value):
        for h in range(heads):
            ref[h * PAD : (h + 1) * PAD, :] = x * head_mask(h, value).astype(BF16)

    def gathered_heads(x):
        return sum(x[h * PAD : (h + 1) * PAD, :] * head_mask(h, 1.0) for h in range(heads))

    def attend_memory():
        spread(qall, qkv[0, mem_rows, :], HD**-0.5)
        p = softmax(nt(qall[...], qkv[1]) + kbias[...])
        pmem[...] = p
        mixed[mem_rows, :] = gathered_heads(nn(p, qkv[2])).astype(BF16)

    def each_part(body):
        for j in range(parts):
            body(j)

    def feed(rows):
        resid = hid[rows, :].astype(F32) + nt(mixed[rows, :], wot[...])
        h1, i1 = normalize(resid)
        hat1[rows, :] = h1
        inv[rows, 0:1] = i1
        norm_one = h1 * gain1 + bias1
        nlow[rows, :] = norm_one.astype(BF16)
        hat2[rows, :] = norm_one

        def step(j):
            inner = nn(nlow[rows, :], wup[j])
            cumulative = 0.5 * (1.0 + lax.erf(inner * 0.7071067811865476))
            density = jnp.exp(-0.5 * inner * inner) * 0.3989422804014327
            a = (inner * cumulative).astype(BF16)
            act[j, rows, :] = a
            slope[j, rows, :] = (cumulative + inner * density).astype(BF16)
            hat2[rows, :] += nt(a, wdnt[j])

        each_part(step)
        h2, i2 = normalize(hat2[rows, :])
        hat2[rows, :] = h2
        inv[rows, 1:2] = i2
        return (h2 * gain2 + bias2).astype(BF16)

    def feed_back(rows, grad_final):
        h2 = hat2[rows, :]
        dnorm[2:3, :] += jnp.sum(grad_final * h2, axis=0, keepdims=True)
        dnorm[3:4, :] += jnp.sum(grad_final, axis=0, keepdims=True)
        g2 = normalize_back(grad_final, h2, inv[rows, 1:2], gain2)
        g2low[rows, :] = g2.astype(BF16)
        gone[rows, :] = g2

        def step(j):
            gi = (nn(g2low[rows, :], wdnt[j]) * slope[j, rows, :].astype(F32)).astype(BF16)
            ginner[j, rows, :] = gi
            gone[rows, :] += nt(gi, wup[j])

        each_part(step)
        grad_norm = gone[rows, :]
        h1 = hat1[rows, :]
        dnorm[0:1, :] += jnp.sum(grad_norm * h1, axis=0, keepdims=True)
        dnorm[1:2, :] += jnp.sum(grad_norm, axis=0, keepdims=True)
        g1 = normalize_back(grad_norm, h1, inv[rows, 0:1], gain1)
        gone[rows, :] = g1
        low = g1.astype(BF16)
        g1low[rows, :] = low
        gmix[rows, :] = nn(low, wot[...]).astype(BF16)

    def memory_keys_back():
        dprob = nt(vall[...], gmix[tok_rows, :]).reshape(heads, PAD, SEG)
        product = gmix[tok_rows, :].astype(F32) * mixed[tok_rows, :].astype(F32)
        high = product.astype(BF16)
        low = (product - high.astype(F32)).astype(BF16)
        row = lax.broadcasted_iota(jnp.int32, (16, width), 0)
        ones = jnp.where(head_of == row, 1.0, 0.0).astype(BF16)
        delta = (nt(ones, high) + nt(ones, low))[0:heads]
        probs_memory = pmemory[...].astype(F32).reshape(heads, PAD, SEG)
        ds = (probs_memory * (dprob - delta[:, None, :])).reshape(heads * PAD, SEG).astype(BF16)
        dk = gathered_heads(nn(ds, qkv[0, tok_rows, :])) * HD**-0.5
        dqkv[1, mem_rows, :] = dk.astype(BF16)
        dqkv[2, mem_rows, :] = gathered_heads(nn(pmemory[...], gmix[tok_rows, :])).astype(BF16)
        dqkv[0, tok_rows, :] = tn(ds, kall[...]).astype(BF16)

    def attend_back():
        for pair in range(pairs):
            lanes = slice(pair * 128, (pair + 1) * 128)
            scaled = gmix[tok_rows, lanes].astype(F32) * pair_scale(pair)
            gmix[tok_rows, lanes] = scaled.astype(BF16)

        @pl.loop(0, pairs)
        def _(pair):
            lanes = pl.ds(pl.multiple_of(pair * 128, 128), 128)
            q = qkv[0, tok_rows, lanes]
            k = qkv[1, tok_rows, lanes]
            v = qkv[2, tok_rows, lanes]
            g = gmix[tok_rows, lanes]
            product = g.astype(F32) * mixed[tok_rows, lanes].astype(F32)
            dqs = []
            dk = None
            dv = None
            for half in range(2):
                e = probs[2 * pair + half]
                gh = g * half_one[half]
                inside = first_half if half == 0 else ~first_half
                delta = jnp.sum(jnp.where(inside, product, 0.0), axis=-1, keepdims=True)
                ds = (e.astype(F32) * (nt(gh, v) - delta)).astype(BF16)
                dv_h = tn(e, gh)
                dk_h = tn(ds, q * half_scaled[half])
                dqs.append(nn(ds, k))
                dk = dk_h if dk is None else dk + dk_h
                dv = dv_h if dv is None else dv + dv_h
            dq = jnp.where(first_half, dqs[0], dqs[1]) * HD**-0.5
            dq += dqkv[0, tok_rows, lanes].astype(F32)
            dqkv[0, tok_rows, lanes] = dq.astype(BF16)
            dqkv[1, tok_rows, lanes] = dk.astype(BF16)
            dqkv[2, tok_rows, lanes] = dv.astype(BF16)

    def more(g, rows, extra):
        dqkv[g, rows, :] = (dqkv[g, rows, :].astype(F32) + extra).astype(BF16)

    def attend_back_memory():
        spread(qall, qkv[0, mem_rows, :], HD**-0.5)
        spread(gall, gmix[mem_rows, :], 1.0)
        dprob = nt(gall[...], qkv[2])
        pf = pmem[...].astype(F32)
        delta = jnp.sum(pf * dprob, axis=-1, keepdims=True)
        ds = (pf * (dprob - delta)).astype(BF16)
        dqkv[0, mem_rows, :] = (gathered_heads(nn(ds, qkv[1])) * HD**-0.5).astype(BF16)
        more(1, mem_rows, tn(ds[:, SEG:], qall[...]))
        more(2, mem_rows, tn(pmem[:, SEG:], gall[...]))
        probs[0, 0 : heads * PAD, :] = ds[:, 0:SEG]

    def attend_back_tokens():
        more(1, tok_rows, tn(probs[0, 0 : heads * PAD, :], qall[...]))
        more(2, tok_rows, tn(pmem[:, 0:SEG], gall[...]))

    def chain_copy(src, dst, slot, peer):
        return remote(src, dst, chain_sem.at[2 * slot], chain_sem.at[2 * slot + 1], (dp, peer))

    forward_copy = chain_copy(mem_send, mem_recv, 0, lax.rem(mp + 1, n))
    backward_copy = chain_copy(gm_send, gm_recv, 1, lax.rem(mp + n - 1, n))

    def take_memory():
        memory = small[4 : 4 + MEM, :]
        memory = jnp.concatenate([memory, jnp.zeros((PAD - MEM, width), F32)], axis=0)
        memory = jnp.where(starts, memory, mem_recv[...].astype(F32))
        hid[mem_rows, :] = memory.astype(BF16)
        project(mem_rows)

    load_tok.wait()
    onward(1)
    for c in range(2):
        project(pl.ds(c * 256, 256))
        onward(1)
    stats[...] = jnp.zeros_like(stats)
    for pair in range(pairs):
        attend_pair(pair)
        if pair == 3:

            @pl.when(mp == 0)
            def _():
                take_memory()
                attend_memory()

        if pair % 2 == 0:
            onward(1)
    onward(len(later))

    @pl.when(mp > 0)
    def _():
        forward_copy.wait_recv()
        take_memory()

    @pl.when((mp > 0) & (mp < n - 1))
    def _():
        attend_memory()

    @pl.when(mp < n - 1)
    def _():
        mem_send[...] = feed(mem_rows)
        forward_copy.start()

    attend_to_memory()

    @pl.loop(0, 2)
    def _(c):
        rows = pl.ds(pl.multiple_of(c * 256, 256), 256)
        lout[rows, :] = feed(rows)

    own = pl.ds(mp * SEG, SEG)
    keep_out = pltpu.make_async_copy(lout.at[tok_rows], lo_hbm.at[own], lo_sem)
    keep_out.start()
    keep_out.wait()
    out_copies = []
    size = SEG // PIECES

    def send_out(first, last):
        for piece in range(first, last):
            for step in (3, 2, 1):
                rows = pl.ds(mp * SEG + piece * size, size)
                copy = remote(lo_hbm.at[rows], lo_hbm.at[rows], lo_send.at[piece, step - 1],
                              lo_recv.at[piece, step - 1], (dp, at["z"][step]))
                copy.start()
                out_copies.append(copy)

    send_out(0, 6)

    dnorm[...] = jnp.zeros_like(dnorm)
    load_cot.wait()

    @pl.loop(0, 2)
    def _(c):
        rows = pl.ds(pl.multiple_of(c * 256, 256), 256)
        feed_back(rows, cot[rows, :].astype(F32))

    def input_grad(rows):
        return (
            gone[rows, :]
            + nt(dqkv[0, rows, :], wqkv[0])
            + nt(dqkv[1, rows, :], wqkv[1])
            + nt(dqkv[2, rows, :], wqkv[2])
        )

    def give_memory_grad():
        gmem = input_grad(mem_rows)
        gm_send[...] = jnp.where(carries, gmem, 0.0).astype(BF16)

        @pl.when(mp > 0)
        def _():
            backward_copy.start()

        dmem[...] = jnp.where(starts, gmem, 0.0)

    memory_keys_back()

    @pl.when(mp == n - 1)
    def _():
        give_memory_grad()

    attend_back()

    @pl.when(mp < n - 1)
    def _():
        backward_copy.wait_recv()
        feed_back(mem_rows, gm_recv[...].astype(F32))
        attend_back_memory()
        give_memory_grad()

    send_out(6, 8)
    cols = width // n
    for i in range(m):
        tiny[i, 0:MEM, :] = dmem[0:MEM, i * part : (i + 1) * part]
        tiny[i, MEM:, :] = dnorm[0:4, i * part : (i + 1) * part]
    dx_copies = []

    def tokens_back():
        @pl.when(mp < n - 1)
        def _():
            attend_back_tokens()

        for c in range(2):
            rows = pl.ds(c * 256, 256)
            g = gone[rows, :].T
            for j in range(3):
                g += nt(wqkv[j], dqkv[j, rows, :])
            g = g.astype(BF16)
            for j in range(n):
                dxs[j, :, rows] = g[j * cols : (j + 1) * cols]

        keep_dx = pltpu.make_async_copy(dxs.at[mp], dx_hbm.at[mp], dx_sem)
        keep_dx.start()
        dx_copies.append(keep_dx)
        for step in range(1, n):
            peer = at['z'][step]
            copy = remote(dxs.at[peer], dx_hbm.at[mp], dx_send.at[step - 1],
                          dx_recv.at[step - 1], (dp, peer))
            copy.start()
            dx_copies.append(copy)

    def in_thirds(body):
        @pl.loop(0, width // 256)
        def _(i):
            body(pl.ds(pl.multiple_of(i * 256, 256), 256))

    def down_grad(j):
        def third(some):
            wdnt[j, some, :] = tn(g2low[:, some], act[j]).astype(BF16)

        in_thirds(third)

    def up_grad(j):
        def third(some):
            wup[j, some, :] = tn(nlow[:, some], ginner[j]).astype(BF16)

        in_thirds(third)

    def attend_grads():
        def third(some):
            wot[some, :] = tn(g1low[:, some], mixed[...]).astype(BF16)
            for g in range(3):
                wqkv[g, some, :] = tn(hid[:, some], dqkv[g]).astype(BF16)

        in_thirds(third)

    if fused:
        finish_gather()
        tiny_start, tiny_end = tiny_steps(at, tiny, tsum, trecv, t_send, t_recv)
        f1, fetch, f2, f3, f4, total_of, finish_scatter = scatter_steps(
            at, (dfull, ufull, afull), firsts, rings, r2x, r2y, r3x, r3y, r4, ssems
        )
        tiny_start(0)
        order = (3, 2, 1, 0)
        for s in range(15):
            if s < 4:
                down_grad(at["z"][order[s]])
            elif s < 8:
                up_grad(at["z"][order[s - 4]])
            elif s == 8:
                tokens_back()
                attend_grads()

                @pl.loop(0, m)
                def _(i):
                    rows = pl.ds(pl.multiple_of(i * part, part), part)
                    w = [wqkv[g, rows, :] if g < 3 else wot[rows, :] for g in range(4)]
                    for j in range(n):
                        lo = j * cols
                        spot = afull.at[j, i // 4, lax.rem(i // 2, 2), lax.rem(i, 2)]
                        for g in range(4):
                            spot[g * part : (g + 1) * part, :] = w[g][:, lo : lo + 128]
                        for g in range(2):
                            spot[(4 + g) * part : (5 + g) * part, :] = jnp.concatenate(
                                [w[2 * g][:, lo + 128 : lo + cols],
                                 w[2 * g + 1][:, lo + 128 : lo + cols]],
                                axis=1,
                            )

            if s < 8:
                send_out(s + 8, s + 9)
            if s < 12:
                f1(s)
            if 1 <= s < 13:
                fetch(s - 1)
            if 1 <= s < 13:
                f2(s - 1)
            if 2 <= s < 14:
                f3(s - 2)
            if 3 <= s:
                f4(s - 3)
            if s < 5:
                tiny_end(s)
                if s < 4:
                    tiny_start(s + 1)
        done = tsum[0, dp]
        dmem_out[...] = done[0:MEM]
        for i in range(4):
            dnorm_out[i][...] = done[MEM + i : MEM + i + 1]
        ddown_out[...] = total_of(0)
        dup_out[...] = total_of(1)
        a = total_of(2)
        for g in range(4):
            edge = a[(4 + g // 2) * part : (5 + g // 2) * part, (g % 2) * HD : (g % 2 + 1) * HD]
            block = jnp.concatenate([a[g * part : (g + 1) * part], edge], axis=1)
            if g < 3:
                dqkv_out[g] = block
            else:
                dout_out[...] = block.T
        finish_scatter()
    else:
        send_out(8, PIECES)
        tokens_back()
        pl.loop(0, parts)(down_grad)
        pl.loop(0, parts)(up_grad)
        attend_grads()
        stores = [
            pltpu.make_async_copy(src, dst, w_sem.at[i])
            for i, (src, dst) in enumerate(zip((wqkv, wot, wup, wdnt), grads_hbm))
        ]
        for store in stores:
            store.start()
        for store in stores:
            store.wait()
    for copy in out_copies + dx_copies:
        copy.wait()

    @pl.when(mp < n - 1)
    def _():
        forward_copy.wait_send()

    @pl.when(mp > 0)
    def _():
        backward_copy.wait_send()


def run_layer(n, m, fused, tokens, cotangent, resets, truncation, key_mask, *rest):
    width = tokens.shape[1]
    parts = n
    heads = width // HD
    part = width // m
    vmem = pl.BlockSpec(memory_space=pltpu.VMEM)
    smem = pl.BlockSpec(memory_space=pltpu.SMEM)
    anyspace = pl.BlockSpec(memory_space=pl.ANY)
    sems = pltpu.SemaphoreType.DMA
    out_shape = [
        jax.ShapeDtypeStruct((n * SEG, width), BF16),
        jax.ShapeDtypeStruct((n, width // n, SEG), BF16),
    ]
    if fused:
        pieces = [(6 * part, 128), (part, width), (part, width)]
        backward = [pieces[2], pieces[1], pieces[0]]
        out_shape += [jax.ShapeDtypeStruct((4, 2, 2) + p, BF16) for p in backward]
        out_shape += [jax.ShapeDtypeStruct(w.shape, F32) for w in rest[5:]]
        out_shape += [jax.ShapeDtypeStruct((MEM, part), F32)]
        out_shape += [jax.ShapeDtypeStruct((1, part), F32)] * 4
        in_rest = [vmem] * len(rest)
        out_specs = [anyspace] * 5 + [vmem] * 9
        first = (
            [pltpu.VMEM((m, 32, part), F32), pltpu.VMEM((32, part), F32),
             pltpu.VMEM(pieces[0], BF16)]
            + [pltpu.VMEM((4, 2, 2, 2) + p, BF16) for p in pieces]
            + gather_sems(3)
            + [sems((m - 1,)), sems((m - 1,))]
            + [pltpu.VMEM((3, width, width), BF16), pltpu.VMEM((width, width), BF16)]
            + [pltpu.VMEM((2, 2) + pieces[0], BF16)]
            + scatter_scratch(backward)
            + [pltpu.VMEM((m, MEM + 4, part), F32), pltpu.VMEM((2, m, MEM + 4, part), F32),
               pltpu.VMEM((5, m, MEM + 4, part), F32), sems((5,)), sems((5,))]
        )
    else:
        shapes = [w.shape for w in rest[1:]]
        out_shape += [jax.ShapeDtypeStruct(s, BF16) for s in shapes]
        out_shape += [jax.ShapeDtypeStruct((m, MEM + 4, part), F32)]
        in_rest = [vmem] + [anyspace] * 4
        out_specs = [anyspace] * 6 + [vmem]
        first = [pltpu.VMEM(s, BF16) for s in shapes]
    row_bf = pltpu.VMEM((ROWS, width), BF16)
    row_f = pltpu.VMEM((ROWS, width), F32)
    one_f = pltpu.VMEM((ROWS, 2), F32)
    wide = pltpu.VMEM((parts, ROWS, width), BF16)
    mem_bf = pltpu.VMEM((PAD, width), BF16)
    all_bf = pltpu.VMEM((heads * PAD, width), BF16)
    return pl.pallas_call(
        functools.partial(layer_kernel, n, m, fused),
        out_shape=tuple(out_shape),
        in_specs=[anyspace, anyspace, smem, smem, vmem] + in_rest,
        out_specs=tuple(out_specs),
        scratch_shapes=first + [
            pltpu.VMEM((1, ROWS), F32), pltpu.VMEM((32, width), F32),
            pltpu.VMEM((heads * PAD, ROWS), BF16), all_bf, all_bf,
            pltpu.VMEM((heads * PAD, SEG), BF16), pltpu.VMEM((SEG, 128), F32),
            row_bf, pltpu.VMEM((SEG, width), BF16), pltpu.VMEM((3, ROWS, width), BF16),
            pltpu.VMEM((heads, SEG, SEG), BF16), row_bf, row_f, one_f, row_bf, wide, wide, row_f,
            row_bf, row_bf, row_bf, pltpu.VMEM((3, ROWS, width), BF16),
            pltpu.VMEM((n, width // n, SEG), BF16),
            pltpu.VMEM((8, width), F32), pltpu.VMEM((PAD, width), F32),
            mem_bf, mem_bf, mem_bf, mem_bf,
            sems((2,)), sems((4,)), sems, sems, sems((PIECES, n - 1)), sems((PIECES, n - 1)), sems((n - 1,)),
            sems((n - 1,)), sems((4,)),
        ],
        compiler_params=pltpu.CompilerParams(
            collective_id=0, has_side_effects=True, vmem_limit_bytes=255 * 2**18
        ),
        cost_estimate=pl.CostEstimate(
            flops=26_000_000_000, bytes_accessed=40_000_000, transcendentals=10_000_000
        ),
    )(tokens, cotangent, resets, truncation, key_mask, *rest)


def finish_kernel(lo_in, dx_in, *refs):
    count = (len(refs) - 5) // 2
    lo_out, dx_out, held, sem_in, sem_out = refs[count], refs[count + 1], *refs[-3:]
    pieces, size = held.shape[:2]
    loads = [
        pltpu.make_async_copy(lo_in.at[pl.ds(i * size, size)], held.at[i], sem_in.at[i])
        for i in range(pieces)
    ]
    stores = [
        pltpu.make_async_copy(held.at[i], lo_out.at[pl.ds(i * size, size)], sem_out.at[i])
        for i in range(pieces)
    ]
    for load in loads:
        load.start()
    for j in range(dx_in.shape[0]):
        dx_out[:, j * SEG : (j + 1) * SEG] = dx_in[j].astype(F32)
    for src, dst in zip(refs[:count], refs[count + 2 : -3]):
        dst[...] = src[...]
    for load, store in zip(loads, stores):
        load.wait()
        store.start()
    for store in stores:
        store.wait()


def finish_outputs(lo, dx, *rest):
    vmem = pl.BlockSpec(memory_space=pltpu.VMEM)
    anyspace = pl.BlockSpec(memory_space=pl.ANY)
    n, cols, rows = dx.shape
    return pl.pallas_call(
        finish_kernel,
        out_shape=(
            jax.ShapeDtypeStruct(lo.shape, lo.dtype),
            jax.ShapeDtypeStruct((cols, n * rows), F32),
            *[jax.ShapeDtypeStruct(r.shape, r.dtype) for r in rest],
        ),
        in_specs=[anyspace] + [vmem] * (1 + len(rest)),
        out_specs=(anyspace,) + (vmem,) * (1 + len(rest)),
        scratch_shapes=[
            pltpu.VMEM((n, lo.shape[0] // n, lo.shape[1]), BF16),
            pltpu.SemaphoreType.DMA((n,)),
            pltpu.SemaphoreType.DMA((n,)),
        ],
        compiler_params=pltpu.CompilerParams(vmem_limit_bytes=60 * 2**20),
    )(lo, dx, *rest)


def shards(
    tokens, cotangent, resets, key_mask, truncation_segments, qkv_weight, out_weight, up_weight,
    down_weight, memory_init, norm1_gain, first_norm_bias, norm2_gain, norm2_bias,
):
    n = lax.axis_size("mp")
    m = lax.axis_size("dp")
    width = tokens.shape[1]
    slots = resets.shape[0]
    rows = width // m
    cols = width // n
    if m == 8 and n == 4 and width == 768:
        out = run_layer(
            n, m, True, tokens, cotangent, resets, truncation_segments,
            key_mask.reshape(slots, SEG), norm1_gain[None], first_norm_bias[None],
            norm2_gain[None], norm2_bias[None], memory_init, qkv_weight, out_weight, up_weight,
            down_weight.T,
        )
        lo, dx, *rest = finish_outputs(*out[:2], *out[5:])
        return (lo, dx.T, *rest[:3], rest[3].T, rest[4], *[d[0] for d in rest[5:]])
    small = jnp.concatenate(
        [norm1_gain[None], first_norm_bias[None], norm2_gain[None], norm2_bias[None], memory_init,
         jnp.zeros((32 - 4 - MEM, rows), BF16)],
        axis=0,
    )
    block = jnp.concatenate([qkv_weight, out_weight.T[None]], axis=0)
    block = lax.all_gather(block, ("mp", "dp"), axis=0)
    block = block.reshape(n, m, 4, rows, cols).transpose(2, 1, 3, 0, 4).reshape(4, width, width)
    wup = lax.all_gather(up_weight, ("mp", "dp"), axis=0).reshape(n, width, -1)
    wdnt = lax.all_gather(down_weight.T, ("mp", "dp"), axis=0).reshape(n, width, -1)
    small = lax.all_gather(small, "dp", axis=1, tiled=True).astype(F32)
    lo, dx, dqkv, dot_w, dup, ddnt, tiny = run_layer(
        n, m, False, tokens, cotangent, resets, truncation_segments, key_mask.reshape(slots, SEG),
        small, block[:3], block[3], wup, wdnt,
    )
    dblock = jnp.concatenate([dqkv, dot_w[None]], axis=0)
    dblock = dblock.reshape(4, m, rows, n, cols).transpose(3, 1, 0, 2, 4)
    dblock = dblock.reshape(n * m, 4, rows, cols)
    dblock = lax.psum_scatter(dblock, ("mp", "dp"), scatter_dimension=0).astype(F32)
    dup = lax.psum_scatter(
        dup.reshape(n * m, rows, -1), ("mp", "dp"), scatter_dimension=0
    ).astype(F32)
    ddnt = lax.psum_scatter(
        ddnt.reshape(n * m, rows, -1), ("mp", "dp"), scatter_dimension=0
    ).astype(F32)
    tiny = lax.psum(tiny, ("mp", "dp"))[lax.axis_index("dp")]
    return (
        lo,
        dx.astype(F32).transpose(0, 2, 1).reshape(n * SEG, cols),
        dblock[:3],
        dblock[3].T,
        dup,
        ddnt.T,
        tiny[:MEM],
        tiny[MEM],
        tiny[MEM + 1],
        tiny[MEM + 2],
        tiny[MEM + 3],
    )


def solution(mesh):
    return jax.shard_map(
        shards,
        mesh=mesh,
        in_specs=(
            P("dp", None), P("dp", None), P("dp"), P("dp"), P(),
            P(None, "dp", "mp"), P("mp", "dp"), P("dp", "mp"), P("mp", "dp"), P(None, "dp"),
            P("dp"), P("dp"), P("dp"), P("dp"),
        ),
        out_specs=(
            P("dp", None), P("dp", "mp"), P(None, "dp", "mp"), P("mp", "dp"), P("dp", "mp"),
            P("mp", "dp"), P(None, "dp"), P("dp"), P("dp"), P("dp"), P("dp"),
        ),
        check_vma=False,
    )
```
